256 devices in a mesh: expert: 16 (over z, core), tensor: 16 (over y, x).
Axes of the slice: x: 4, y: 4, z: 8, core: 2. Of those that a mesh axis runs over, the one named last changes fastest.
Arguments:
- hidden_in: bfloat16 [256, 4096], P(('expert', 'tensor')), may hold values from -6 to 6
- x_stream: bfloat16 [256, 8192], P('expert', 'tensor'), may hold values from -6 to 6
- z_stream: bfloat16 [256, 8192], P('expert', 'tensor'), may hold values from -6 to 6
- conv_state: bfloat16 [256, 3, 8192], P('expert', None, 'tensor'), may hold values from -6 to 6
- ssm_state: float32 [256, 16, 8192], P('expert', None, 'tensor'), may hold values from -3 to 3
- conv_weight: bfloat16 [4, 8192], P(None, 'tensor'), may hold values from -3 to 3
- conv_bias: float32 [8192], P('tensor'), may hold values from -3 to 3
- x_weight: bfloat16 [8192, 544], P('tensor'), may hold values from -0.0625 to 0.0625
- dt_weight: bfloat16 [512, 8192], P(None, 'tensor'), may hold values from -0.25 to 0.25
- dt_bias: float32 [8192], P('tensor'), may hold values from -4 to -1
- a_log: float32 [16, 8192], P(None, 'tensor'), may hold values from 0 to 2.8
- skip_gain: float32 [8192], P('tensor'), may hold values from 0.5 to 1.5
- out_weight: bfloat16 [16, 512, 4096], P('tensor', 'expert'), may hold values from -0.0625 to 0.0625
- norm_gain: float32 [4096], replicated, may hold values from 0.5 to 1.5
- route_ids: int32 [256, 2], replicated, may hold values from 0 to 7, as said below
- route_weights: float32 [256, 2], replicated, may hold values from 0.1 to 0.9
- gate_proj: bfloat16 [16, 4096, 6144], P('expert', None, 'tensor'), may hold values from -0.09375 to 0.09375
- up_proj: bfloat16 [16, 4096, 6144], P('expert', None, 'tensor'), may hold values from -0.09375 to 0.09375
- down_proj: bfloat16 [16, 6144, 4096], P('expert', 'tensor'), may hold values from -0.0546875 to 0.0546875
Outputs:
- layer_output: bfloat16 [256, 4096], P(('expert', 'tensor'))
- new_conv_state: bfloat16 [256, 3, 8192], P('expert', None, 'tensor')
- new_ssm_state: float32 [256, 16, 8192], P('expert', None, 'tensor')
The draws below stay inside these ranges and needn't reach their ends.
Inputs may be any that keep to these rules, and one draw needn't show every extreme that they name: `route_ids`: each request names two different experts. Among the 16 requests of each index of expert (rows g * 16 to (g + 1) * 16 - 1) no expert is named more than 12 times, and one expert, the same for every index, is named exactly 12 times.
All inputs are finite; a program needn't handle non-finite values.
Results may differ from the reference program's by a relative error of at most 0.025.
Values may be sent and summed in bfloat16 or wider, within the bound.
A program may use at most 64 MiB of HBM per device.

```python
import jax
import jax.numpy as jnp
from jax import lax

D = 4096
DI = 8192
NS = 16
DTR = 512
KC = 4
EXPERTS = 8
FFE = 12288
GROUP = 2
REQ = 16
REQS = 256
C_GRP = 12
CAP = 192
N_EXPERT = 16
N_TENSOR = 16


def draw_route_ids(key, part):
    key = jax.random.fold_in(key, 5)
    subkeys = jax.random.split(key, 6)
    others = EXPERTS - 1
    hot_expert = jax.random.randint(subkeys[0], (), 0, EXPERTS)
    rank_table = jax.vmap(lambda sub: jax.random.permutation(sub, REQ))(jax.random.split(subkeys[1], N_EXPERT))
    offset = jax.random.randint(subkeys[2], (N_EXPERT, 1), 0, others)
    partner = (offset + rank_table) % others
    first_pick = jax.random.randint(subkeys[3], (N_EXPERT, REQ), 0, others)
    stride = jax.random.randint(subkeys[4], (N_EXPERT, REQ), 1, others)
    second = (first_pick + stride) % others
    is_hot = rank_table < C_GRP
    column_one = jnp.where(is_hot, hot_expert, (hot_expert + 1 + first_pick) % EXPERTS)
    column_two = jnp.where(is_hot, (hot_expert + 1 + partner) % EXPERTS, (hot_expert + 1 + second) % EXPERTS)
    swapped = jax.random.randint(subkeys[5], (N_EXPERT, REQ), 0, 2) == 1
    leading = jnp.where(swapped, column_two, column_one)
    trailing = jnp.where(swapped, column_one, column_two)
    return jnp.stack([leading, trailing], axis=-1).reshape(REQS, 2).astype(jnp.int32)


def block_scale(own_key, extent, pieces, low, largest):
    level = 1.0
    for position, blocks in pieces:
        heights = jax.random.uniform(jax.random.fold_in(jax.random.fold_in(own_key, 6), position), (blocks,), jnp.float32, low / len(pieces), largest / len(pieces))
        level = level * jnp.repeat(jnp.exp(heights), extent[position] // blocks).reshape((-1,) + (1,) * (len(extent) - 1 - position))
    return level


def scatter_about(stream_key, extent, spread, reach, shards=(), kind=jnp.bfloat16):
    values = spread * jax.random.normal(stream_key, extent, jnp.float32)
    if shards:
        values = values * block_scale(stream_key, extent, shards, -0.22, 0.18)
    return jnp.clip(values, -reach, reach).astype(kind)


def setup_inputs(seed: int = 0) -> dict:
    key_list = jax.random.split(jax.random.key(seed), 20)
    hidden_in = scatter_about(key_list[0], (REQS, D), 1.0, 6.0, ((0, 256),))
    x_stream = scatter_about(key_list[1], (REQS, DI), 1.0, 6.0, ((0, 16), (1, 16)))
    z_stream = scatter_about(key_list[2], (REQS, DI), 1.0, 6.0, ((0, 16), (1, 16)))
    conv_state = scatter_about(key_list[3], (REQS, KC - 1, DI), 1.0, 6.0, ((0, 16), (2, 16)))
    ssm_state = scatter_about(key_list[4], (REQS, NS, DI), 0.5, 3.0, ((0, 16), (2, 16)), jnp.float32)
    conv_weight = scatter_about(key_list[5], (KC, DI), KC ** -0.5, 3.0, ((1, 16),))
    conv_bias = scatter_about(key_list[6], (DI,), 0.5, 3.0, ((0, 16),), jnp.float32)
    x_weight = scatter_about(key_list[7], (DI, DTR + 2 * NS), DI ** -0.5, 0.0625, ((0, 16),))
    dt_weight = scatter_about(key_list[8], (DTR, DI), DTR ** -0.5, 0.25, ((1, 16),))
    dt_bias = jnp.clip(-4.0 + 3.0 * jax.random.uniform(key_list[9], (DI,), jnp.float32) ** block_scale(key_list[9], (DI,), ((0, 16),), -0.2, 0.2), -4.0, -1.0)
    a_log = jnp.clip(2.8 * jax.random.uniform(key_list[10], (NS, DI), jnp.float32) ** block_scale(key_list[10], (NS, DI), ((1, 16),), -0.2, 0.2), 0.0, 2.8)
    skip_gain = jnp.clip(0.5 + 1.0 * jax.random.uniform(key_list[11], (DI,), jnp.float32) ** block_scale(key_list[11], (DI,), ((0, 16),), -0.2, 0.2), 0.5, 1.5)
    out_weight = scatter_about(key_list[12], (N_TENSOR, DI // N_TENSOR, D), DI ** -0.5, 0.0625, ((0, 16), (1, 16)))
    norm_gain = jnp.clip(1.0 + 0.1 * jax.random.normal(key_list[13], (D,), jnp.float32), 0.5, 1.5)
    route_ids = draw_route_ids(jax.random.fold_in(key_list[19], 71), 0)
    route_weights = jnp.clip(jax.random.uniform(key_list[15], (REQS, 2), jnp.float32, 0.1, 0.9), 0.1, 0.9)
    gate_proj = scatter_about(key_list[16], (N_EXPERT, D, FFE // GROUP), D ** -0.5, 0.09375, ((0, 16), (2, 16)))
    up_proj = scatter_about(key_list[17], (N_EXPERT, D, FFE // GROUP), D ** -0.5, 0.09375, ((0, 16), (2, 16)))
    down_proj = scatter_about(key_list[18], (N_EXPERT, FFE // GROUP, D), FFE ** -0.5, 0.0546875, ((0, 16), (1, 16)))
    return dict(hidden_in=hidden_in, x_stream=x_stream, z_stream=z_stream, conv_state=conv_state, ssm_state=ssm_state, conv_weight=conv_weight, conv_bias=conv_bias, x_weight=x_weight, dt_weight=dt_weight, dt_bias=dt_bias, a_log=a_log, skip_gain=skip_gain, out_weight=out_weight, norm_gain=norm_gain, route_ids=route_ids, route_weights=route_weights, gate_proj=gate_proj, up_proj=up_proj, down_proj=down_proj)


def rms_norm(values, gain):
    wide = values.astype(jnp.float32)
    scale = lax.rsqrt(lax.optimization_barrier(jnp.mean(wide * wide, axis=-1, keepdims=True)) + 1e-05)
    return (wide * scale * gain).astype(jnp.bfloat16)

def expert_mlp(rows_in, w_gate, w_up, w_down):
    gate_part = jnp.dot(rows_in, w_gate, preferred_element_type=jnp.float32)
    up_part = jnp.dot(rows_in, w_up, preferred_element_type=jnp.float32)
    active = (jax.nn.silu(gate_part) * up_part).astype(jnp.bfloat16)
    return jnp.dot(active, w_down, preferred_element_type=jnp.float32)

def reference(hidden_in, x_stream, z_stream, conv_state, ssm_state, conv_weight, conv_bias, x_weight, dt_weight, dt_bias, a_log, skip_gain, out_weight, norm_gain, route_ids, route_weights, gate_proj, up_proj, down_proj):
    window = jnp.concatenate([conv_state, x_stream[:, None, :]], axis=1)
    conv_sum = lax.optimization_barrier(jnp.sum(window.astype(jnp.float32) * conv_weight.astype(jnp.float32)[None], axis=1)) + conv_bias
    conv_out = jax.nn.silu(conv_sum).astype(jnp.bfloat16)
    new_conv_state = window[:, 1:, :]
    selective = jnp.dot(conv_out, x_weight, preferred_element_type=jnp.float32)
    dt_low = selective[:, :DTR].astype(jnp.bfloat16)
    b_part = selective[:, DTR:DTR + NS]
    c_part = selective[:, DTR + NS:]
    step_size = jax.nn.softplus(jnp.dot(dt_low, dt_weight, preferred_element_type=jnp.float32) + dt_bias)
    decay_rate = jnp.exp(-step_size[:, None, :] * jnp.exp(a_log)[None])
    inputs = conv_out.astype(jnp.float32)
    new_ssm_state = decay_rate * ssm_state + (step_size * inputs)[:, None, :] * b_part[:, :, None]
    readout = lax.optimization_barrier(jnp.sum(new_ssm_state * c_part[:, :, None], axis=1)) + skip_gain * inputs
    mixer_out = (readout * jax.nn.silu(z_stream.astype(jnp.float32))).astype(jnp.bfloat16)
    mixed_sum = jnp.dot(mixer_out, out_weight.reshape(DI, D), preferred_element_type=jnp.float32)
    residual = (hidden_in.astype(jnp.float32) + mixed_sum).astype(jnp.bfloat16)
    normed = rms_norm(residual, norm_gain)
    row_ids = jnp.arange(REQS, dtype=jnp.int32)
    expert_total = jnp.zeros((REQS, D), jnp.float32)
    for expert in range(EXPERTS):
        hit_mask = route_ids == expert
        member = jnp.any(hit_mask, axis=1)
        weight = lax.optimization_barrier(jnp.sum(jnp.where(hit_mask, route_weights, 0.0), axis=1))
        slot_place = (jnp.cumsum(member.astype(jnp.int32)) - 1).astype(jnp.int32)
        target = jnp.where(member, slot_place, CAP).astype(jnp.int32)
        slot_rows = jnp.zeros((CAP + 1,), jnp.int32).at[target].set(row_ids)[:CAP]
        w_gate = jnp.concatenate([gate_proj[expert * GROUP + half_index] for half_index in range(GROUP)], axis=1)
        w_up = jnp.concatenate([up_proj[expert * GROUP + half_index] for half_index in range(GROUP)], axis=1)
        w_down = jnp.concatenate([down_proj[expert * GROUP + half_index] for half_index in range(GROUP)], axis=0)
        result = expert_mlp(normed[slot_rows], w_gate, w_up, w_down)
        gathered = result[jnp.clip(slot_place, 0, CAP - 1)]
        expert_total = expert_total + jnp.where(member[:, None], weight[:, None] * gathered, 0.0)
    layer_output = (residual.astype(jnp.float32) + expert_total).astype(jnp.bfloat16)
    return (layer_output, new_conv_state, new_ssm_state)
```

```python
import jax
import jax.numpy as jnp
from jax import lax
from jax.experimental import pallas as pl
from jax.experimental.pallas import tpu as pltpu
from jax.sharding import PartitionSpec as P

F32 = jnp.float32
BF16 = jnp.bfloat16
MESH = pl.DeviceIdType.MESH

PROJ_X, PROJ_Y, WOUT, HIDDEN, MIXED, OUTRED, RESID, ROWS1, ROWS2, ROWS3, PAIR, RED1, RED2, FINAL = range(14)


def layer_kernel(
    x_ref, z_ref, cs_ref, cw_ref, cb_ref, xw_ref, dtb_ref, alog_ref, skip_ref, gain_ref, ids_ref, rw_ref, hid_ref,
    dtw_hbm, ssm_hbm, ow_hbm, gate_hbm, up_hbm, down_hbm,
    out_ref, ncs_ref, nssm_ref,
    dtw, ssm, wg, wu, wd, ow,
    proj, proj_x, proj_y, hid_out, hid_in, readout, mix, outb, outr, res, resrow, xn, acc_g, acc_u, actw, wrow, perm,
    osend, opair, own, red1, tsum, red2, vrow, vsend, final_in,
    ssem, rsem, lsem,
):
    e = lax.axis_index("expert")
    t = lax.axis_index("tensor")
    y, x = lax.div(t, 4), lax.rem(t, 4)
    c = lax.rem(e, 2)
    mate = e + 1 - 2 * c
    expert = lax.div(e, 2)

    def rcopy(src, dst, phase, to, frm, device):
        return pltpu.make_async_remote_copy(
            src_ref=src, dst_ref=dst, send_sem=ssem.at[phase, to], recv_sem=rsem.at[phase, frm],
            device_id=device, device_id_type=MESH,
        )

    def others(n, me, body):
        def step(d, carry):
            body(lax.rem(me + d, n))
            return carry
        lax.fori_loop(1, n, step, 0)

    bar = pltpu.get_barrier_semaphore()
    others(16, e, lambda o: pl.semaphore_signal(bar, inc=1, device_id=(o, t), device_id_type=MESH))
    others(16, t, lambda o: pl.semaphore_signal(bar, inc=1, device_id=(e, o), device_id_type=MESH))

    def lcopy(src, dst, i):
        return pltpu.make_async_copy(src, dst, lsem.at[i])

    dtw_copy = lcopy(dtw_hbm, dtw, 0)
    ssm_copy = lcopy(ssm_hbm, ssm, 1)
    my_cols = pl.ds(pl.multiple_of(e * 256, 256), 256)
    ow_copy = lcopy(ow_hbm.at[0, :, my_cols], ow.at[e], 2)
    dtw_copy.start()
    ssm_copy.start()
    ow_copy.start()
    weights = []
    for q in range(4):
        weights.append((
            lcopy(gate_hbm.at[0, pl.ds(q * 1024, 1024), :], wg.at[q], 3 + q),
            lcopy(up_hbm.at[0, pl.ds(q * 1024, 1024), :], wu.at[q], 7 + q),
            lcopy(down_hbm.at[0, :, pl.ds(q * 1024, 1024)], wd.at[q], 11 + q),
        ))

    state = cs_ref[...].astype(F32)
    taps = cw_ref[...].astype(F32)
    newest = x_ref[...].astype(F32)
    window = [state[:, 0, :], state[:, 1, :], state[:, 2, :], newest]
    conv_sum = sum(window[k] * taps[k : k + 1, :] for k in range(4)) + cb_ref[...]
    conv_out = jax.nn.silu(conv_sum).astype(BF16)
    inputs = conv_out.astype(F32)
    part = jnp.dot(conv_out, xw_ref[...], preferred_element_type=F32)
    proj[0] = jnp.zeros((16, 640), BF16)
    proj[0, :, 0:544] = part.astype(BF16)

    pl.semaphore_wait(bar, 30)

    def proj_x_copy(o):
        return rcopy(proj.at[0], proj_x.at[x], PROJ_X, o, x, (e, y * 4 + o))

    others(4, x, lambda o: proj_x_copy(o).start())

    hidden = hid_ref[...].astype(F32)
    for k in range(16):
        hid_out[k] = hidden[:, 256 * k : 256 * (k + 1)]
    hid_in[e] = hid_out[e]

    def wout_copy(o):
        cols = pl.ds(pl.multiple_of(o * 256, 256), 256)
        return rcopy(ow_hbm.at[0, :, cols], ow.at[e], WOUT, o, e, (o, t))

    def hidden_copy(o):
        return rcopy(hid_out.at[o], hid_in.at[e], HIDDEN, o, e, (o, t))

    others(16, e, lambda o: wout_copy(o).start())
    ncs_ref[...] = jnp.concatenate([state[:, 1:, :], newest[:, None, :]], axis=1).astype(BF16)

    others(4, x, lambda o: rcopy(proj.at[0], proj_x.at[o], PROJ_X, o, o, (e, y * 4 + o)).wait_recv())
    total = proj[0].astype(F32)
    for d in range(1, 4):
        total = total + proj_x[lax.rem(x + d, 4)].astype(F32)
    proj[1] = total.astype(BF16)

    def proj_y_copy(o):
        return rcopy(proj.at[1], proj_y.at[y], PROJ_Y, o, y, (e, o * 4 + x))

    others(4, y, lambda o: proj_y_copy(o).start())
    others(16, e, lambda o: hidden_copy(o).start())
    for group in weights:
        for copy in group:
            copy.start()

    row = lax.broadcasted_iota(jnp.int32, (256, 256), 0)
    col = lax.broadcasted_iota(jnp.int32, (256, 256), 1)
    perm[...] = jnp.where(col == lax.rem(row, 16) * 16 + lax.div(row, 16), 1.0, 0.0).astype(BF16)
    hit = jnp.where(ids_ref[...] == expert, rw_ref[...], 0.0)
    wide = jnp.broadcast_to(jnp.sum(hit, axis=1, keepdims=True), (256, 128))
    high = wide.astype(BF16)
    rest = wide - high.astype(F32)
    mid = rest.astype(BF16)
    low = (rest - mid.astype(F32)).astype(BF16)
    wrow[...] = (
        jnp.dot(perm[...], high, preferred_element_type=F32)
        + jnp.dot(perm[...], mid, preferred_element_type=F32)
        + jnp.dot(perm[...], low, preferred_element_type=F32)
    )
    decay = -jnp.exp(alog_ref[...])
    gate_z = jax.nn.silu(z_ref[...].astype(F32))
    dtw_copy.wait()
    ssm_copy.wait()
    others(4, x, lambda o: proj_x_copy(o).wait_send())

    others(4, y, lambda o: rcopy(proj.at[1], proj_y.at[o], PROJ_Y, o, o, (e, o * 4 + x)).wait_recv())
    total = proj[1].astype(F32)
    for d in range(1, 4):
        total = total + proj_y[lax.rem(y + d, 4)].astype(F32)

    step_size = jax.nn.softplus(
        jnp.dot(total[:, 0:512].astype(BF16), dtw[...], preferred_element_type=F32) + dtb_ref[...]
    )
    maps = total[:, 512:640].T
    b_map, c_map = maps[0:16, :], maps[16:32, :]
    driven = step_size * inputs
    for r in range(16):
        new = jnp.exp(step_size[r : r + 1, :] * decay) * ssm[r] + driven[r : r + 1, :] * b_map[:, r : r + 1]
        nssm_ref[r] = new
        readout[r : r + 1, :] = jnp.sum(new * c_map[:, r : r + 1], axis=0, keepdims=True)
    mix[e] = ((readout[...] + skip_ref[...] * inputs) * gate_z).astype(BF16)

    def mix_copy(o):
        return rcopy(mix.at[e], mix.at[e], MIXED, o, e, (o, t))

    others(16, e, lambda o: mix_copy(o).start())
    others(4, y, lambda o: proj_y_copy(o).wait_send())
    others(16, e, lambda o: wout_copy(o).wait_send())
    others(16, e, lambda o: hidden_copy(o).wait_send())
    ow_copy.wait()
    others(16, e, lambda o: rcopy(ow.at[e], ow.at[o], WOUT, o, o, (o, t)).wait_recv())
    others(16, e, lambda o: rcopy(hid_out.at[o], hid_in.at[o], HIDDEN, o, o, (o, t)).wait_recv())
    others(16, e, lambda o: rcopy(mix.at[e], mix.at[o], MIXED, o, o, (o, t)).wait_recv())
    ordered = jnp.dot(perm[...], mix[...].reshape(256, 512), preferred_element_type=F32).astype(BF16)
    mixed = jnp.dot(ordered, ow[...].reshape(512, 256), preferred_element_type=F32)
    outb[...] = mixed.astype(BF16).reshape(16, 16, 256)

    def out_copy(o):
        return rcopy(outb.at[o], outr.at[t], OUTRED, o, t, (e, o))

    others(16, t, lambda o: out_copy(o).start())
    outr[t] = outb[t]
    others(16, e, lambda o: mix_copy(o).wait_send())
    others(16, t, lambda o: rcopy(outb.at[o], outr.at[o], OUTRED, o, o, (e, o)).wait_recv())
    res[e] = (jnp.sum(outr[...].astype(F32), axis=0) + hid_in[...].reshape(16, 256)).astype(BF16)

    def res_copy(o):
        return rcopy(res.at[e], res.at[e], RESID, o, e, (o, t))

    others(16, e, lambda o: res_copy(o).start())
    others(16, t, lambda o: out_copy(o).wait_send())
    others(16, e, lambda o: rcopy(res.at[e], res.at[o], RESID, o, o, (o, t)).wait_recv())
    squares = jnp.zeros((16, 256), F32)
    for b in range(16):
        piece = res[b].astype(F32)
        squares = squares + piece * piece
    scale = lax.rsqrt(jnp.sum(squares, axis=1, keepdims=True) * (1.0 / 4096) + 1e-5)
    for i in range(8):
        gain = gain_ref[:, pl.ds(pl.multiple_of(c * 2048 + i * 256, 256), 256)]
        value = (res[8 * c + i].astype(F32) * scale * gain).astype(BF16)
        xn[2 * c + i // 4, y, x, :, (i % 4) * 256 : (i % 4 + 1) * 256] = value

    q0, q1 = 2 * c, 2 * c + 1

    def rows1_x(o, frm):
        return rcopy(xn.at[q0, y, x], xn.at[q0, y, frm], ROWS1, o, frm, (e, y * 4 + o))

    def rows1_y(o, frm):
        return rcopy(xn.at[q1, y, x], xn.at[q1, frm, x], ROWS1, 4 + o, 4 + frm, (e, o * 4 + x))

    def rows2_y(o, frm):
        return rcopy(xn.at[q0, y], xn.at[q0, frm], ROWS2, o, frm, (e, o * 4 + x))

    def rows2_x(o, frm):
        return rcopy(xn.at[q1, :, x], xn.at[q1, :, frm], ROWS2, 4 + o, 4 + frm, (e, y * 4 + o))

    def rows3_0(q, o):
        return rcopy(xn.at[q, o], xn.at[q, o], ROWS3, o, o, (mate, t))

    def rows3_1(q, o):
        return rcopy(xn.at[q, :, o], xn.at[q, :, o], ROWS3, 4 + o, 4 + o, (mate, t))

    others(4, x, lambda o: rows1_x(o, x).start())
    others(4, y, lambda o: rows1_y(o, y).start())
    others(16, e, lambda o: res_copy(o).wait_send())
    mine = lax.broadcasted_iota(jnp.int32, (16, 256), 0) == e
    for b in range(16):
        resrow[b : b + 1, :] = jnp.sum(jnp.where(mine, res[b].astype(F32), 0.0), axis=0, keepdims=True)
    others(4, x, lambda o: rows1_x(o, o).wait_recv())
    others(4, y, lambda o: rows2_y(o, y).start())
    rows3_0(q0, y).start()
    others(4, y, lambda o: rows1_y(o, o).wait_recv())
    others(4, x, lambda o: rows2_x(o, x).start())
    rows3_1(q1, x).start()
    for group in weights:
        for copy in group:
            copy.wait()
    others(4, x, lambda o: rows1_x(o, x).wait_send())
    others(4, y, lambda o: rows1_y(o, y).wait_send())

    def forward(d, carry):
        oy, ox = lax.rem(y + d, 4), lax.rem(x + d, 4)
        rows2_y(oy, oy).wait_recv()
        rows3_0(q0, oy).start()
        rows2_x(ox, ox).wait_recv()
        rows3_1(q1, ox).start()
        return carry

    lax.fori_loop(1, 4, forward, 0)

    acc_g[...] = jnp.zeros((256, 384), F32)
    acc_u[...] = jnp.zeros((256, 384), F32)

    def project(q):
        rows = xn[q].reshape(256, 1024)
        acc_g[...] += jnp.dot(rows, wg[q], preferred_element_type=F32)
        acc_u[...] += jnp.dot(rows, wu[q], preferred_element_type=F32)

    def project_half(first):
        def step(s, carry):
            project(first + s)
            return carry
        lax.fori_loop(0, 2, step, 0)

    project_half(q0)
    p0 = 2 - 2 * c

    def mate_rows(o, carry):
        rows3_0(p0, o).wait_recv()
        rows3_1(p0 + 1, o).wait_recv()
        return carry

    lax.fori_loop(0, 4, mate_rows, 0)
    project_half(p0)
    weight = jnp.concatenate([wrow[...]] * 3, axis=1)
    actw[...] = (jax.nn.silu(acc_g[...]) * acc_u[...] * weight).astype(BF16)

    def pair_copy(s):
        return rcopy(osend.at[s], opair.at[s], PAIR, s, s, (mate, t))

    def down_mate(s, carry):
        value = jnp.dot(actw[...], wd[p0 + s], preferred_element_type=F32)
        osend[s] = value.astype(BF16).reshape(4, 4, 16, 1024)
        pair_copy(s).start()
        return carry

    lax.fori_loop(0, 2, down_mate, 0)

    def red1_x(o, frm):
        return rcopy(own.at[0, :, o], red1.at[0, frm], RED1, o, frm, (e, y * 4 + o))

    def red1_y(o, frm):
        return rcopy(own.at[1, o], red1.at[1, frm], RED1, 4 + o, 4 + frm, (e, o * 4 + x))

    def down_own(s):
        value = jnp.dot(actw[...], wd[q0 + s], preferred_element_type=F32)
        pair_copy(s).wait_recv()
        own[s] = (value + opair[s].astype(F32).reshape(256, 1024)).astype(BF16).reshape(4, 4, 16, 1024)

    down_own(0)
    others(4, x, lambda o: red1_x(o, x).start())
    down_own(1)
    others(4, y, lambda o: red1_y(o, y).start())

    others(4, y, lambda o: rows2_y(o, y).wait_send())
    others(4, x, lambda o: rows2_x(o, x).wait_send())

    def rows3_sent(o, carry):
        rows3_0(q0, o).wait_send()
        rows3_1(q1, o).wait_send()
        return carry

    lax.fori_loop(0, 4, rows3_sent, 0)
    pair_copy(0).wait_send()
    pair_copy(1).wait_send()

    def red2_y(o, frm):
        return rcopy(tsum.at[0, o], red2.at[0, frm], RED2, o, frm, (e, o * 4 + x))

    def red2_x(o, frm):
        return rcopy(tsum.at[1, o], red2.at[1, frm], RED2, 4 + o, 4 + frm, (e, y * 4 + o))

    others(4, x, lambda o: red1_x(o, o).wait_recv())
    value = own[0, :, x].astype(F32)
    for d in range(1, 4):
        value = value + red1[0, lax.rem(x + d, 4)].astype(F32)
    tsum[0] = value.astype(BF16)
    others(4, y, lambda o: red2_y(o, y).start())
    others(4, y, lambda o: red1_y(o, o).wait_recv())
    value = own[1, y].astype(F32)
    for d in range(1, 4):
        value = value + red1[1, lax.rem(y + d, 4)].astype(F32)
    tsum[1] = value.astype(BF16)
    others(4, x, lambda o: red2_x(o, x).start())
    others(4, x, lambda o: red1_x(o, x).wait_send())
    others(4, y, lambda o: red1_y(o, y).wait_send())

    others(4, y, lambda o: red2_y(o, o).wait_recv())
    first = tsum[0, y].astype(F32)
    for d in range(1, 4):
        first = first + red2[0, lax.rem(y + d, 4)].astype(F32)
    others(4, x, lambda o: red2_x(o, o).wait_recv())
    second = tsum[1, x].astype(F32)
    for d in range(1, 4):
        second = second + red2[1, lax.rem(x + d, 4)].astype(F32)

    for k in range(8):
        vrow[:, k, :] = first[:, 128 * k : 128 * (k + 1)]
        vrow[:, 8 + k, :] = second[:, 128 * k : 128 * (k + 1)]
    vsend[...] = vrow[...].astype(BF16)

    def final_copy(o):
        return rcopy(vsend.at[o], final_in.at[e], FINAL, o, e, (o, t))

    others(16, e, lambda o: final_copy(o).start())
    final_in[e] = vsend[e]
    others(4, y, lambda o: red2_y(o, y).wait_send())
    others(4, x, lambda o: red2_x(o, x).wait_send())
    others(16, e, lambda o: rcopy(vsend.at[o], final_in.at[o], FINAL, o, o, (o, t)).wait_recv())
    for half in range(2):
        value = final_in[half].astype(F32)
        for k in range(1, 8):
            value = value + final_in[2 * k + half].astype(F32)
        for k in range(16):
            m = 16 * half + k
            tail = resrow[m // 2 : m // 2 + 1, (m % 2) * 128 : (m % 2 + 1) * 128]
            out_ref[:, 128 * m : 128 * (m + 1)] = value[k : k + 1, :] + tail
    others(16, e, lambda o: final_copy(o).wait_send())


def local(
    hidden_in,
    x_stream,
    z_stream,
    conv_state,
    ssm_state,
    conv_weight,
    conv_bias,
    x_weight,
    dt_weight,
    dt_bias,
    a_log,
    skip_gain,
    out_weight,
    norm_gain,
    route_ids,
    route_weights,
    gate_proj,
    up_proj,
    down_proj,
):
    vmem = pl.BlockSpec(memory_space=pltpu.VMEM)
    hbm = pl.BlockSpec(memory_space=pl.ANY)
    row, new_conv_state, new_ssm_state = pl.pallas_call(
        layer_kernel,
        out_shape=(
            jax.ShapeDtypeStruct((1, 4096), F32),
            jax.ShapeDtypeStruct((16, 3, 512), BF16),
            jax.ShapeDtypeStruct((16, 16, 512), F32),
        ),
        in_specs=[vmem] * 13 + [hbm] * 6,
        out_specs=(vmem, vmem, vmem),
        scratch_shapes=[
            pltpu.VMEM((512, 512), BF16),
            pltpu.VMEM((16, 16, 512), F32),
            pltpu.VMEM((4, 1024, 384), BF16),
            pltpu.VMEM((4, 1024, 384), BF16),
            pltpu.VMEM((4, 384, 1024), BF16),
            pltpu.VMEM((16, 32, 256), BF16),
            pltpu.VMEM((2, 16, 640), BF16),
            pltpu.VMEM((4, 16, 640), BF16),
            pltpu.VMEM((4, 16, 640), BF16),
            pltpu.VMEM((16, 1, 256), F32),
            pltpu.VMEM((16, 1, 256), F32),
            pltpu.VMEM((16, 512), F32),
            pltpu.VMEM((16, 16, 512), BF16),
            pltpu.VMEM((16, 16, 256), BF16),
            pltpu.VMEM((16, 16, 256), BF16),
            pltpu.VMEM((16, 16, 256), BF16),
            pltpu.VMEM((16, 256), F32),
            pltpu.VMEM((4, 4, 4, 16, 1024), BF16),
            pltpu.VMEM((256, 384), F32),
            pltpu.VMEM((256, 384), F32),
            pltpu.VMEM((256, 384), BF16),
            pltpu.VMEM((256, 128), F32),
            pltpu.VMEM((256, 256), BF16),
            pltpu.VMEM((2, 4, 4, 16, 1024), BF16),
            pltpu.VMEM((2, 4, 4, 16, 1024), BF16),
            pltpu.VMEM((2, 4, 4, 16, 1024), BF16),
            pltpu.VMEM((2, 4, 4, 16, 1024), BF16),
            pltpu.VMEM((2, 4, 16, 1024), BF16),
            pltpu.VMEM((2, 4, 16, 1024), BF16),
            pltpu.VMEM((16, 16, 128), F32),
            pltpu.VMEM((16, 16, 128), BF16),
            pltpu.VMEM((16, 16, 128), BF16),
            pltpu.SemaphoreType.DMA((14, 16)),
            pltpu.SemaphoreType.DMA((14, 16)),
            pltpu.SemaphoreType.DMA((16,)),
        ],
        compiler_params=pltpu.CompilerParams(
            collective_id=0, has_side_effects=True, vmem_limit_bytes=48 * 1024 * 1024
        ),
        name="layer",
    )(
        x_stream, z_stream, conv_state, conv_weight, conv_bias[None], x_weight, dt_bias[None], a_log,
        skip_gain[None], norm_gain[None], route_ids, route_weights, hidden_in,
        dt_weight, ssm_state, out_weight, gate_proj, up_proj, down_proj,
    )
    return (row.astype(BF16), new_conv_state, new_ssm_state)


def solution(mesh):
    return jax.shard_map(
        local,
        mesh=mesh,
        in_specs=(
            P(("expert", "tensor"), None),
            P("expert", "tensor"),
            P("expert", "tensor"),
            P("expert", None, "tensor"),
            P("expert", None, "tensor"),
            P(None, "tensor"),
            P("tensor"),
            P("tensor", None),
            P(None, "tensor"),
            P("tensor"),
            P(None, "tensor"),
            P("tensor"),
            P("tensor", "expert", None),
            P(),
            P(),
            P(),
            P("expert", None, "tensor"),
            P("expert", None, "tensor"),
            P("expert", "tensor", None),
        ),
        out_specs=(
            P(("expert", "tensor"), None),
            P("expert", None, "tensor"),
            P("expert", None, "tensor"),
        ),
        check_vma=False,
    )
```

```python
import jax
import jax.numpy as jnp
from jax import lax
from jax.experimental import pallas as pl
from jax.experimental.pallas import tpu as pltpu
from jax.sharding import PartitionSpec as P

F32 = jnp.float32
BF16 = jnp.bfloat16
MESH = pl.DeviceIdType.MESH

(
    PROJ, WOUT_M, WOUT, HID_M, HID, DOWN_M, MIX, MIX_M, OUTRED, RESID, STAT, SCALE,
    ROWS1, ROWS2, ROWS3, ACT, RED1, RED2, FINAL, FINAL_M,
) = range(20)


def layer_kernel(
    x_hbm, z_hbm, cs_hbm, cw_hbm, cb_hbm, xw_hbm, dtb_hbm, alog_hbm, skip_hbm, gain_hbm, ids_hbm, rw_hbm, hid_hbm,
    dtw_hbm, ssm_hbm, ow_hbm, gate_hbm, up_hbm, down_hbm,
    out_ref, ncs_hbm, nssm_hbm,
    ncs_ref, nssm_ref, x_ref, z_ref, cs_ref, cw_ref, cb_ref, xw_ref, dtb_ref, alog_ref, skip_ref, gain_ref, ids_ref, rw_ref, hid_ref,
    dtw, ssm, wg, wu, wd, wd_mate, owh, ow,
    proj, proj_in, hid_out, hidh, hid_in, readout, mix, outb, outr, res, stat, scales, resrow, xn, acc_g, acc_u,
    actw, act_mate, wrow, perm, own, red1, tsum, red2, vrow, vsend, final_in, fbuf, fmate,
    ssem, rsem, lsem,
):
    e = lax.axis_index("expert")
    t = lax.axis_index("tensor")
    y, x = lax.div(t, 4), lax.rem(t, 4)
    z, c = lax.div(e, 2), lax.rem(e, 2)
    m = 1 - c
    mate = 2 * z + m
    q0, q1 = 2 * c, 2 * c + 1
    p0 = 2 * m

    def rcopy(src, dst, phase, to, frm, device):
        return pltpu.make_async_remote_copy(
            src_ref=src, dst_ref=dst, send_sem=ssem.at[phase, to], recv_sem=rsem.at[phase, frm],
            device_id=device, device_id_type=MESH,
        )

    def others(n, me, body):
        def step(d, carry):
            body(lax.rem(me + d, n))
            return carry
        lax.fori_loop(1, n, step, 0)

    def at_z(o):
        return (2 * o + c, t)

    def at_x(o):
        return (e, y * 4 + o)

    def at_y(o):
        return (e, o * 4 + x)

    def half(which):
        return pl.ds(pl.multiple_of(which * 2048, 2048), 2048)

    def lcopy(src, dst, i):
        return pltpu.make_async_copy(src, dst, lsem.at[i])

    early = [
        lcopy(src, dst, i) for i, (src, dst) in enumerate((
            (x_hbm, x_ref), (cs_hbm, cs_ref), (cw_hbm, cw_ref), (cb_hbm, cb_ref), (xw_hbm, xw_ref),
        ))
    ]
    later = [
        lcopy(src, dst, 5 + i) for i, (src, dst) in enumerate((
            (hid_hbm, hid_ref), (dtw_hbm, dtw), (ssm_hbm, ssm), (ids_hbm, ids_ref), (rw_hbm, rw_ref),
            (z_hbm, z_ref), (dtb_hbm, dtb_ref), (alog_hbm, alog_ref), (skip_hbm, skip_ref), (gain_hbm, gain_ref),
        ))
    ]
    weights = []
    for q in range(4):
        weights.append(lcopy(gate_hbm.at[0, pl.ds(q * 1024, 1024), :], wg.at[q], 16 + q))
        weights.append(lcopy(up_hbm.at[0, pl.ds(q * 1024, 1024), :], wu.at[q], 20 + q))

    def down_cols(which, s):
        return down_hbm.at[0, :, pl.ds(pl.multiple_of(which * 2048 + s * 1024, 1024), 1024)]

    for s in range(2):
        weights.append(lcopy(down_cols(c, s), wd.at[s], 24 + s))
    own_weight = lcopy(ow_hbm.at[0, :, half(c)], owh.at[c], 15)
    for copy in early:
        copy.start()
    own_weight.start()

    def greet(device):
        pl.semaphore_signal(bar, inc=1, device_id=device, device_id_type=MESH)

    bar = pltpu.get_barrier_semaphore()
    others(16, t, lambda o: greet((e, o)))
    others(8, z, lambda o: greet(at_z(o)))
    greet((mate, t))

    for copy in early:
        copy.wait()
    state = cs_ref[...].astype(F32)
    taps = cw_ref[...].astype(F32)
    newest = x_ref[...].astype(F32)
    window = [state[0], state[1], state[2], newest]
    conv_sum = sum(window[k] * taps[k : k + 1, :] for k in range(4)) + cb_ref[...]
    conv_out = jax.nn.silu(conv_sum).astype(BF16)
    inputs = conv_out.astype(F32)
    part = lax.dot_general(
        conv_out, xw_ref[...], (((1,), (1,)), ((), ())), preferred_element_type=F32
    )
    proj[...] = jnp.zeros((16, 640), BF16)
    proj[:, 0:544] = part.astype(BF16)

    pl.semaphore_wait(bar, 23)

    def wout_copy(o):
        cols = pl.ds(pl.multiple_of(o * 256, 256), 256)
        return rcopy(owh.at[:, :, cols], ow.at[z], WOUT, o, z, at_z(o))

    def wout_from(o):
        return rcopy(ow.at[o], ow.at[o], WOUT, o, o, at_z(o))

    def proj_copy(o):
        return rcopy(proj, proj_in.at[t], PROJ, o, t, (e, o))

    wout_mate = rcopy(ow_hbm.at[0, :, half(m)], owh.at[c], WOUT_M, 0, 0, (mate, t))
    wout_from_mate = rcopy(ow_hbm.at[0, :, half(m)], owh.at[m], WOUT_M, 0, 0, (mate, t))
    wout_mate.start()
    others(16, t, lambda o: proj_copy(o).start())
    proj_in[t] = proj[...]
    wout_from_mate.wait_recv()
    own_weight.wait()
    others(8, z, lambda o: wout_copy(o).start())

    hid_mate = rcopy(hid_out.at[pl.ds(8 * m, 8)], hidh.at[:, c], HID_M, 0, 0, (mate, t))
    hid_from_mate = rcopy(hid_out.at[pl.ds(8 * m, 8)], hidh.at[:, m], HID_M, 0, 0, (mate, t))

    def down_mate(s):
        return rcopy(down_cols(m, s), wd_mate.at[s], DOWN_M, s, s, (mate, t))

    for copy in later:
        copy.start()
    for copy in later:
        copy.wait()
    hidden = hid_ref[...].astype(F32)
    for k in range(16):
        hid_out[k] = hidden[:, 256 * k : 256 * (k + 1)]
    hid_mate.start()
    hidh[:, c] = hid_out[pl.ds(8 * c, 8)]
    ncs_ref[0] = cs_ref[1]
    ncs_ref[1] = cs_ref[2]
    ncs_ref[2] = x_ref[...]
    ncs_copy = lcopy(ncs_ref, ncs_hbm, 26)
    ncs_copy.start()

    ow[z] = owh[:, :, pl.ds(pl.multiple_of(z * 256, 256), 256)]

    def hid_copy(o):
        return rcopy(hidh.at[o], hid_in.at[z], HID, o, z, at_z(o))

    def hid_from(o):
        return rcopy(hidh.at[o], hid_in.at[o], HID, o, o, at_z(o))

    row = lax.broadcasted_iota(jnp.int32, (256, 256), 0)
    col = lax.broadcasted_iota(jnp.int32, (256, 256), 1)
    chosen = col == lax.rem(row, 16) * 16 + lax.div(row, 16)
    perm[...] = jnp.where(chosen, 1.0, 0.0).astype(BF16)
    hit = jnp.sum(jnp.where(ids_ref[...] == z, rw_ref[...], 0.0), axis=0, keepdims=True)
    picked = jnp.sum(jnp.where(chosen, hit, 0.0), axis=1, keepdims=True)
    wrow[...] = jnp.broadcast_to(picked, (256, 128))
    decay = -jnp.exp(alog_ref[...])
    gate_z = jax.nn.silu(z_ref[...].astype(F32))
    wout_mate.wait_send()
    hid_mate.wait_send()

    others(16, t, lambda o: rcopy(proj, proj_in.at[o], PROJ, o, o, (e, o)).wait_recv())
    total = jnp.sum(proj_in[...].astype(F32), axis=0)

    step_size = jax.nn.softplus(
        jnp.dot(total[:, 0:512].astype(BF16), dtw[...], preferred_element_type=F32) + dtb_ref[...]
    )
    maps = total[:, 512:640].T
    b_map, c_map = maps[0:16, :], maps[16:32, :]
    driven = step_size * inputs
    for r in range(16):
        new = jnp.exp(step_size[r : r + 1, :] * decay) * ssm[r] + driven[r : r + 1, :] * b_map[:, r : r + 1]
        nssm_ref[r] = new
        readout[r : r + 1, :] = jnp.sum(new * c_map[:, r : r + 1], axis=0, keepdims=True)
    nssm_copy = lcopy(nssm_ref, nssm_hbm, 27)
    nssm_copy.start()
    mix[e] = ((readout[...] + skip_ref[...] * inputs) * gate_z).astype(BF16)

    def mix_copy(o):
        return rcopy(mix.at[e], mix.at[e], MIX, o, z, at_z(o))

    def mix_from(o):
        return rcopy(mix.at[2 * o + c], mix.at[2 * o + c], MIX, o, o, at_z(o))

    def mix_to_mate(o):
        return rcopy(mix.at[2 * o + c], mix.at[2 * o + c], MIX_M, o, o, (mate, t))

    def mix_from_mate(o):
        return rcopy(mix.at[2 * o + m], mix.at[2 * o + m], MIX_M, o, o, (mate, t))

    others(8, z, lambda o: mix_copy(o).start())
    mix_to_mate(z).start()
    hid_from_mate.wait_recv()
    others(8, z, lambda o: hid_copy(o).start())
    hid_in[z] = hidh[z]
    for copy in weights:
        copy.start()
    others(8, z, lambda o: wout_from(o).wait_recv())

    def mix_pass(o):
        mix_from(o).wait_recv()
        mix_to_mate(o).start()

    others(8, z, mix_pass)
    mix_from_mate(z).wait_recv()
    others(8, z, lambda o: mix_from_mate(o).wait_recv())
    ordered = jnp.dot(perm[...], mix[...].reshape(256, 512), preferred_element_type=F32).astype(BF16)
    mixed = jnp.dot(ordered, ow[...].reshape(512, 256), preferred_element_type=F32)
    outb[...] = mixed.astype(BF16).reshape(16, 16, 256)

    def out_copy(o):
        return rcopy(outb.at[o], outr.at[t], OUTRED, o, t, (e, o))

    others(16, t, lambda o: out_copy(o).start())
    outr[t] = outb[t]
    down_mate(0).start()
    down_mate(1).start()
    others(16, t, lambda o: proj_copy(o).wait_send())
    others(8, z, lambda o: wout_copy(o).wait_send())
    others(8, z, lambda o: hid_copy(o).wait_send())
    others(8, z, lambda o: hid_from(o).wait_recv())
    others(8, z, lambda o: mix_copy(o).wait_send())
    mix_to_mate(z).wait_send()
    others(8, z, lambda o: mix_to_mate(o).wait_send())
    others(16, t, lambda o: rcopy(outb.at[o], outr.at[o], OUTRED, o, o, (e, o)).wait_recv())
    res[z] = (jnp.sum(outr[...].astype(F32), axis=0) + hid_in[...].reshape(16, 256)).astype(BF16)

    def res_copy(o):
        return rcopy(res.at[z], res.at[z], RESID, o, z, at_z(o))

    others(8, z, lambda o: res_copy(o).start())
    others(16, t, lambda o: out_copy(o).wait_send())
    others(8, z, lambda o: rcopy(res.at[o], res.at[o], RESID, o, o, at_z(o)).wait_recv())
    for b in range(8):
        gain = gain_ref[:, pl.ds(pl.multiple_of(c * 2048 + b * 256, 256), 256)]
        value = (res[b].astype(F32) * gain).astype(BF16)
        xn[2 * c + b // 4, y, x, :, (b % 4) * 256 : (b % 4 + 1) * 256] = value

    def rows1_x(o, frm):
        return rcopy(xn.at[q0, y, x], xn.at[q0, y, frm], ROWS1, o, frm, at_x(o))

    def rows1_y(o, frm):
        return rcopy(xn.at[q1, y, x], xn.at[q1, frm, x], ROWS1, 4 + o, 4 + frm, at_y(o))

    def rows2_y(o, frm):
        return rcopy(xn.at[q0, y], xn.at[q0, frm], ROWS2, o, frm, at_y(o))

    def rows2_x(o, frm):
        return rcopy(xn.at[q1, :, x], xn.at[q1, :, frm], ROWS2, 4 + o, 4 + frm, at_x(o))

    def rows3_0(q, o):
        return rcopy(xn.at[q, o], xn.at[q, o], ROWS3, o, o, (mate, t))

    def rows3_1(q, o):
        return rcopy(xn.at[q, :, o], xn.at[q, :, o], ROWS3, 4 + o, 4 + o, (mate, t))

    others(4, x, lambda o: rows1_x(o, x).start())
    others(4, y, lambda o: rows1_y(o, y).start())
    squares = jnp.zeros((16, 256), F32)
    for b in range(8):
        piece = res[b].astype(F32)
        squares = squares + piece * piece
    sums = jnp.broadcast_to(jnp.sum(squares, axis=1, keepdims=True), (16, 128)).T
    stat[0] = jnp.zeros((1, 128), F32)
    stat[0, :, 0:16] = sums[0:1, :]
    stat_copy = rcopy(stat.at[0], stat.at[1], STAT, 0, 0, (mate, t))
    stat_copy.start()
    others(8, z, lambda o: res_copy(o).wait_send())
    stat_copy.wait()
    scales[t] = lax.rsqrt((stat[0] + stat[1]) * (1.0 / 4096) + 1e-5)

    def scale_copy(o):
        return rcopy(scales.at[t], scales.at[t], SCALE, o, t, (e, o))

    others(16, t, lambda o: scale_copy(o).start())
    place = lax.broadcasted_iota(jnp.int32, (16, 256), 0)
    for k in range(2):
        mine = place == 2 * z + k
        for b in range(8):
            resrow[k, b : b + 1, :] = jnp.sum(jnp.where(mine, res[b].astype(F32), 0.0), axis=0, keepdims=True)
    others(4, x, lambda o: rows1_x(o, o).wait_recv())
    others(4, y, lambda o: rows2_y(o, y).start())
    rows3_0(q0, y).start()
    others(4, y, lambda o: rows1_y(o, o).wait_recv())
    others(4, x, lambda o: rows2_x(o, x).start())
    rows3_1(q1, x).start()
    for copy in weights:
        copy.wait()
    for s in range(2):
        down_mate(s).wait()
    others(4, x, lambda o: rows1_x(o, x).wait_send())
    others(4, y, lambda o: rows1_y(o, y).wait_send())

    others(16, t, lambda o: rcopy(scales.at[o], scales.at[o], SCALE, o, o, (e, o)).wait_recv())
    lane = lax.broadcasted_iota(jnp.int32, (16, 16, 128), 2)
    slot = lax.broadcasted_iota(jnp.int32, (16, 16, 128), 1)
    picked = jnp.where(lane == slot, jnp.broadcast_to(scales[...], (16, 16, 128)), 0.0).reshape(256, 128)
    scale = jnp.broadcast_to(jnp.sum(picked, axis=1, keepdims=True), (256, 384))

    def forward(d, carry):
        oy, ox = lax.rem(y + d, 4), lax.rem(x + d, 4)
        rows2_y(oy, oy).wait_recv()
        rows3_0(q0, oy).start()
        rows2_x(ox, ox).wait_recv()
        rows3_1(q1, ox).start()
        return carry

    lax.fori_loop(1, 4, forward, 0)

    acc_g[...] = jnp.zeros((256, 384), F32)
    acc_u[...] = jnp.zeros((256, 384), F32)

    def project(q):
        rows = xn[q].reshape(256, 1024)
        acc_g[...] += jnp.dot(rows, wg[q], preferred_element_type=F32)
        acc_u[...] += jnp.dot(rows, wu[q], preferred_element_type=F32)

    def project_half(first):
        def step(s, carry):
            project(first + s)
            return carry
        lax.fori_loop(0, 2, step, 0)

    project_half(q0)

    def mate_rows(o, carry):
        rows3_0(p0, o).wait_recv()
        rows3_1(p0 + 1, o).wait_recv()
        return carry

    lax.fori_loop(0, 4, mate_rows, 0)
    project_half(p0)
    weight = jnp.concatenate([wrow[...]] * 3, axis=1)
    actw[...] = (jax.nn.silu(acc_g[...] * scale) * (acc_u[...] * scale) * weight).astype(BF16)

    act_copy = rcopy(actw, act_mate, ACT, 0, 0, (mate, t))
    act_copy.start()

    def red1_x(o, frm):
        return rcopy(own.at[0, :, o], red1.at[0, frm], RED1, o, frm, at_x(o))

    def red1_y(o, frm):
        return rcopy(own.at[1, o], red1.at[1, frm], RED1, 4 + o, 4 + frm, at_y(o))

    value = jnp.dot(actw[...], wd[0], preferred_element_type=F32)
    act_copy.wait()
    value = value + jnp.dot(act_mate[...], wd_mate[0], preferred_element_type=F32)
    own[0] = value.astype(BF16).reshape(4, 4, 16, 1024)
    others(4, x, lambda o: red1_x(o, x).start())
    value = jnp.dot(actw[...], wd[1], preferred_element_type=F32)
    value = value + jnp.dot(act_mate[...], wd_mate[1], preferred_element_type=F32)
    own[1] = value.astype(BF16).reshape(4, 4, 16, 1024)
    others(4, y, lambda o: red1_y(o, y).start())

    others(16, t, lambda o: scale_copy(o).wait_send())
    others(4, y, lambda o: rows2_y(o, y).wait_send())
    others(4, x, lambda o: rows2_x(o, x).wait_send())

    def rows3_sent(o, carry):
        rows3_0(q0, o).wait_send()
        rows3_1(q1, o).wait_send()
        return carry

    lax.fori_loop(0, 4, rows3_sent, 0)

    def red2_y(o, frm):
        return rcopy(tsum.at[0, o], red2.at[0, frm], RED2, o, frm, at_y(o))

    def red2_x(o, frm):
        return rcopy(tsum.at[1, o], red2.at[1, frm], RED2, 4 + o, 4 + frm, at_x(o))

    others(4, x, lambda o: red1_x(o, o).wait_recv())
    value = own[0, :, x].astype(F32)
    for d in range(1, 4):
        value = value + red1[0, lax.rem(x + d, 4)].astype(F32)
    tsum[0] = value.astype(BF16)
    others(4, y, lambda o: red2_y(o, y).start())
    others(4, y, lambda o: red1_y(o, o).wait_recv())
    value = own[1, y].astype(F32)
    for d in range(1, 4):
        value = value + red1[1, lax.rem(y + d, 4)].astype(F32)
    tsum[1] = value.astype(BF16)
    others(4, x, lambda o: red2_x(o, x).start())
    others(4, x, lambda o: red1_x(o, x).wait_send())
    others(4, y, lambda o: red1_y(o, y).wait_send())

    others(4, y, lambda o: red2_y(o, o).wait_recv())
    first = tsum[0, y].astype(F32)
    for d in range(1, 4):
        first = first + red2[0, lax.rem(y + d, 4)].astype(F32)
    others(4, x, lambda o: red2_x(o, o).wait_recv())
    second = tsum[1, x].astype(F32)
    for d in range(1, 4):
        second = second + red2[1, lax.rem(x + d, 4)].astype(F32)

    for k in range(8):
        vrow[:, k, :] = first[:, 128 * k : 128 * (k + 1)]
        vrow[:, 8 + k, :] = second[:, 128 * k : 128 * (k + 1)]
    vsend[...] = vrow[...].astype(BF16).reshape(8, 2, 16, 128)

    def final_copy(o):
        return rcopy(vsend.at[o], final_in.at[z], FINAL, o, z, at_z(o))

    others(8, z, lambda o: final_copy(o).start())
    final_in[z] = vsend[z]
    others(4, y, lambda o: red2_y(o, y).wait_send())
    others(4, x, lambda o: red2_x(o, x).wait_send())
    others(8, z, lambda o: rcopy(vsend.at[o], final_in.at[o], FINAL, o, o, at_z(o)).wait_recv())
    rows = jnp.sum(final_in[...].astype(F32), axis=0)
    for k in range(2):
        for b in range(16):
            tail = resrow[k, b // 2 : b // 2 + 1, (b % 2) * 128 : (b % 2 + 1) * 128]
            fbuf[k, :, 128 * b : 128 * (b + 1)] = rows[k, b : b + 1, :] + tail
    final_mate = rcopy(fbuf.at[m], fmate, FINAL_M, 0, 0, (mate, t))
    final_mate.start()
    out_ref[:, half(c)] = fbuf[c]
    others(8, z, lambda o: final_copy(o).wait_send())
    final_mate.wait()
    ncs_copy.wait()
    nssm_copy.wait()
    out_ref[:, half(m)] = fmate[...]


def finish_kernel(row, ncs, nssm, row_out, ncs_out, nssm_out, row_in, ncs_in, nssm_in, sem):
    copies = [
        pltpu.make_async_copy(src, dst, sem.at[k])
        for k, (src, dst) in enumerate((
            (nssm, nssm_in), (ncs, ncs_in), (row, row_in), (nssm_in, nssm_out), (ncs_in, ncs_out),
        ))
    ]
    for k in range(3):
        copies[k].start()
    for k in range(2):
        copies[k].wait()
        copies[3 + k].start()
    copies[2].wait()
    row_out[...] = row_in[...].astype(BF16)
    copies[3].wait()
    copies[4].wait()


def local(
    hidden_in,
    x_stream,
    z_stream,
    conv_state,
    ssm_state,
    conv_weight,
    conv_bias,
    x_weight,
    dt_weight,
    dt_bias,
    a_log,
    skip_gain,
    out_weight,
    norm_gain,
    route_ids,
    route_weights,
    gate_proj,
    up_proj,
    down_proj,
):
    vmem = pl.BlockSpec(memory_space=pltpu.VMEM)
    hbm = pl.BlockSpec(memory_space=pltpu.HBM)
    row, new_conv_state, new_ssm_state = pl.pallas_call(
        layer_kernel,
        out_shape=(
            jax.ShapeDtypeStruct((1, 4096), F32),
            jax.ShapeDtypeStruct((3, 16, 512), BF16),
            jax.ShapeDtypeStruct((16, 16, 512), F32),
        ),
        in_specs=[hbm] * 19,
        out_specs=(vmem, hbm, hbm),
        scratch_shapes=[
            pltpu.VMEM((3, 16, 512), BF16),
            pltpu.VMEM((16, 16, 512), F32),
            pltpu.VMEM((16, 512), BF16),
            pltpu.VMEM((16, 512), BF16),
            pltpu.VMEM((3, 16, 512), BF16),
            pltpu.VMEM((4, 512), BF16),
            pltpu.VMEM((1, 512), F32),
            pltpu.VMEM((544, 512), BF16),
            pltpu.VMEM((1, 512), F32),
            pltpu.VMEM((16, 512), F32),
            pltpu.VMEM((1, 512), F32),
            pltpu.VMEM((1, 4096), F32),
            pltpu.VMEM((2, 256), jnp.int32),
            pltpu.VMEM((2, 256), F32),
            pltpu.VMEM((1, 4096), BF16),
            pltpu.VMEM((512, 512), BF16),
            pltpu.VMEM((16, 16, 512), F32),
            pltpu.VMEM((4, 1024, 384), BF16),
            pltpu.VMEM((4, 1024, 384), BF16),
            pltpu.VMEM((2, 384, 1024), BF16),
            pltpu.VMEM((2, 384, 1024), BF16),
            pltpu.VMEM((2, 32, 2048), BF16),
            pltpu.VMEM((8, 2, 32, 256), BF16),
            pltpu.VMEM((16, 640), BF16),
            pltpu.VMEM((16, 16, 640), BF16),
            pltpu.VMEM((16, 1, 256), F32),
            pltpu.VMEM((8, 2, 1, 256), F32),
            pltpu.VMEM((8, 2, 1, 256), F32),
            pltpu.VMEM((16, 512), F32),
            pltpu.VMEM((16, 16, 512), BF16),
            pltpu.VMEM((16, 16, 256), BF16),
            pltpu.VMEM((16, 16, 256), BF16),
            pltpu.VMEM((8, 16, 256), BF16),
            pltpu.VMEM((2, 1, 128), F32),
            pltpu.VMEM((16, 1, 128), F32),
            pltpu.VMEM((2, 8, 256), F32),
            pltpu.VMEM((4, 4, 4, 16, 1024), BF16),
            pltpu.VMEM((256, 384), F32),
            pltpu.VMEM((256, 384), F32),
            pltpu.VMEM((256, 384), BF16),
            pltpu.VMEM((256, 384), BF16),
            pltpu.VMEM((256, 128), F32),
            pltpu.VMEM((256, 256), BF16),
            pltpu.VMEM((2, 4, 4, 16, 1024), BF16),
            pltpu.VMEM((2, 4, 4, 16, 1024), BF16),
            pltpu.VMEM((2, 4, 16, 1024), BF16),
            pltpu.VMEM((2, 4, 16, 1024), BF16),
            pltpu.VMEM((16, 16, 128), F32),
            pltpu.VMEM((8, 2, 16, 128), BF16),
            pltpu.VMEM((8, 2, 16, 128), BF16),
            pltpu.VMEM((2, 1, 2048), F32),
            pltpu.VMEM((1, 2048), F32),
            pltpu.SemaphoreType.DMA((20, 16)),
            pltpu.SemaphoreType.DMA((20, 16)),
            pltpu.SemaphoreType.DMA((28,)),
        ],
        compiler_params=pltpu.CompilerParams(
            collective_id=0, has_side_effects=True, vmem_limit_bytes=58 * 1024 * 1024
        ),
        name="layer",
    )(
        x_stream, z_stream, conv_state.transpose(1, 0, 2), conv_weight, conv_bias[None], x_weight.T, dt_bias[None],
        a_log, skip_gain[None], norm_gain[None], route_ids.T, route_weights.T, hidden_in,
        dt_weight, ssm_state, out_weight, gate_proj, up_proj, down_proj,
    )
    row, new_conv_state, new_ssm_state = pl.pallas_call(
        finish_kernel,
        out_shape=(
            jax.ShapeDtypeStruct((1, 4096), BF16),
            jax.ShapeDtypeStruct((3, 16, 512), BF16),
            jax.ShapeDtypeStruct((16, 16, 512), F32),
        ),
        in_specs=[hbm] * 3,
        out_specs=(vmem, hbm, hbm),
        scratch_shapes=[
            pltpu.VMEM((1, 4096), F32),
            pltpu.VMEM((3, 16, 512), BF16),
            pltpu.VMEM((16, 16, 512), F32),
            pltpu.SemaphoreType.DMA((5,)),
        ],
        compiler_params=pltpu.CompilerParams(vmem_limit_bytes=58 * 1024 * 1024),
        name="finish",
    )(row, new_conv_state, new_ssm_state)
    return (row, new_conv_state.transpose(1, 0, 2), new_ssm_state)


def solution(mesh):
    return jax.shard_map(
        local,
        mesh=mesh,
        in_specs=(
            P(("expert", "tensor"), None),
            P("expert", "tensor"),
            P("expert", "tensor"),
            P("expert", None, "tensor"),
            P("expert", None, "tensor"),
            P(None, "tensor"),
            P("tensor"),
            P("tensor", None),
            P(None, "tensor"),
            P("tensor"),
            P(None, "tensor"),
            P("tensor"),
            P("tensor", "expert", None),
            P(),
            P(),
            P(),
            P("expert", None, "tensor"),
            P("expert", None, "tensor"),
            P("expert", "tensor", None),
        ),
        out_specs=(
            P(("expert", "tensor"), None),
            P("expert", None, "tensor"),
            P("expert", None, "tensor"),
        ),
        check_vma=False,
    )
```

```python
import jax
import jax.numpy as jnp
from jax import lax
from jax.experimental import pallas as pl
from jax.experimental.pallas import tpu as pltpu
from jax.sharding import PartitionSpec as P

F32 = jnp.float32
BF16 = jnp.bfloat16
MESH = pl.DeviceIdType.MESH

(
    PROJ, WOUT_M, WOUT, HID_M, HID, DOWN_M, MIX, MIX_M, OUTRED, RESID, STAT, SCALE,
    ROWS1, ROWS2, ROWS3, ACT, RED1, RED2, FINAL,
) = range(19)


def layer_kernel(
    x_hbm, z_hbm, cs_hbm, cw_hbm, cb_hbm, xw_hbm, dtb_hbm, alog_hbm, skip_hbm, gain_hbm, ids_hbm, rw_hbm, hid_hbm,
    dtw_hbm, ssm_hbm, ow_hbm, gate_hbm, up_hbm, down_hbm,
    out_ref, ncs_ref, nssm_ref,
    x_ref, z_ref, cs_ref, cw_ref, cb_ref, xw_ref, dtb_ref, alog_ref, skip_ref, gain_ref, ids_ref, rw_ref, hid_ref,
    dtw, ssm, wg, wu, wd, wd_mate, owh, ow,
    proj, proj_in, hid_out, hidh, hid_in, readout, mix, outb, outr, res, stat, scales, resrow, xn, acc_g, acc_u,
    actw, act_mate, wrow, perm, own, red1, tsum, red2, vrow, vsend, final_in,
    ssem, rsem, lsem,
):
    e = lax.axis_index("expert")
    t = lax.axis_index("tensor")
    y, x = lax.div(t, 4), lax.rem(t, 4)
    z, c = lax.div(e, 2), lax.rem(e, 2)
    m = 1 - c
    mate = 2 * z + m
    q0, q1 = 2 * c, 2 * c + 1
    p0 = 2 * m

    def rcopy(src, dst, phase, to, frm, device):
        return pltpu.make_async_remote_copy(
            src_ref=src, dst_ref=dst, send_sem=ssem.at[phase, to], recv_sem=rsem.at[phase, frm],
            device_id=device, device_id_type=MESH,
        )

    def others(n, me, body):
        def step(d, carry):
            body(lax.rem(me + d, n))
            return carry
        lax.fori_loop(1, n, step, 0)

    def at_z(o):
        return (2 * o + c, t)

    def at_x(o):
        return (e, y * 4 + o)

    def at_y(o):
        return (e, o * 4 + x)

    def half(which):
        return pl.ds(pl.multiple_of(which * 2048, 2048), 2048)

    def lcopy(src, dst, i):
        return pltpu.make_async_copy(src, dst, lsem.at[i])

    early = [
        lcopy(src, dst, i) for i, (src, dst) in enumerate((
            (x_hbm, x_ref), (cs_hbm, cs_ref), (cw_hbm, cw_ref), (cb_hbm, cb_ref),
        ))
    ]
    later = [
        lcopy(src, dst, 5 + i) for i, (src, dst) in enumerate((
            (hid_hbm, hid_ref), (dtw_hbm, dtw), (ssm_hbm, ssm), (ids_hbm, ids_ref), (rw_hbm, rw_ref),
            (z_hbm, z_ref), (dtb_hbm, dtb_ref), (alog_hbm, alog_ref), (skip_hbm, skip_ref), (gain_hbm, gain_ref),
        ))
    ]
    weights = []
    for q in range(4):
        weights.append(lcopy(gate_hbm.at[0, pl.ds(q * 1024, 1024), :], wg.at[q], 16 + q))
        weights.append(lcopy(up_hbm.at[0, pl.ds(q * 1024, 1024), :], wu.at[q], 20 + q))

    def down_cols(which, s):
        return down_hbm.at[0, :, pl.ds(pl.multiple_of(which * 2048 + s * 1024, 1024), 1024)]

    for s in range(2):
        weights.append(lcopy(down_cols(c, s), wd.at[s], 24 + s))
    for k in range(4):
        part = pl.ds(k * 128, 128 if k < 3 else 160)
        early.append(lcopy(xw_hbm.at[part], xw_ref.at[part], 28 + k))
    own_weight = lcopy(ow_hbm.at[0, :, half(c)], owh.at[c], 15)
    for copy in early:
        copy.start()
    own_weight.start()

    def greet(device):
        pl.semaphore_signal(bar, inc=1, device_id=device, device_id_type=MESH)

    bar = pltpu.get_barrier_semaphore()
    others(16, t, lambda o: greet((e, o)))
    others(8, z, lambda o: greet(at_z(o)))
    greet((mate, t))

    for copy in early:
        copy.wait()
    state = cs_ref[...].astype(F32)
    taps = cw_ref[...].astype(F32)
    newest = x_ref[...].astype(F32)
    window = [state[0], state[1], state[2], newest]
    conv_sum = sum(window[k] * taps[k : k + 1, :] for k in range(4)) + cb_ref[...]
    conv_out = jax.nn.silu(conv_sum).astype(BF16)
    inputs = conv_out.astype(F32)
    part = lax.dot_general(
        conv_out, xw_ref[...], (((1,), (1,)), ((), ())), preferred_element_type=F32
    )
    proj[...] = jnp.zeros((16, 640), BF16)
    proj[:, 0:544] = part.astype(BF16)

    pl.semaphore_wait(bar, 23)

    def wout_copy(o):
        cols = pl.ds(pl.multiple_of(o * 256, 256), 256)
        return rcopy(owh.at[:, :, cols], ow.at[z], WOUT, o, z, at_z(o))

    def wout_from(o):
        return rcopy(ow.at[o], ow.at[o], WOUT, o, o, at_z(o))

    def proj_copy(o):
        return rcopy(proj, proj_in.at[t], PROJ, o, t, (e, o))

    wout_mate = rcopy(ow_hbm.at[0, :, half(m)], owh.at[c], WOUT_M, 0, 0, (mate, t))
    wout_from_mate = rcopy(ow_hbm.at[0, :, half(m)], owh.at[m], WOUT_M, 0, 0, (mate, t))
    wout_mate.start()
    others(16, t, lambda o: proj_copy(o).start())
    proj_in[t] = proj[...]
    wout_from_mate.wait_recv()
    own_weight.wait()
    others(8, z, lambda o: wout_copy(o).start())

    hid_mate = rcopy(hid_out.at[pl.ds(8 * m, 8)], hidh.at[:, c], HID_M, 0, 0, (mate, t))
    hid_from_mate = rcopy(hid_out.at[pl.ds(8 * m, 8)], hidh.at[:, m], HID_M, 0, 0, (mate, t))

    def down_mate(s):
        return rcopy(down_cols(m, s), wd_mate.at[s], DOWN_M, s, s, (mate, t))

    for copy in later:
        copy.start()
    for copy in weights:
        copy.start()
    for copy in later:
        copy.wait()
    hidden = hid_ref[...].astype(F32)
    for k in range(16):
        hid_out[k] = hidden[:, 256 * k : 256 * (k + 1)]
    hid_mate.start()
    hidh[:, c] = hid_out[pl.ds(8 * c, 8)]
    ncs_ref[0] = cs_ref[1]
    ncs_ref[1] = cs_ref[2]
    ncs_ref[2] = x_ref[...]

    ow[z] = owh[:, :, pl.ds(pl.multiple_of(z * 256, 256), 256)]

    def hid_copy(o):
        return rcopy(hidh.at[o], hid_in.at[z], HID, o, z, at_z(o))

    def hid_from(o):
        return rcopy(hidh.at[o], hid_in.at[o], HID, o, o, at_z(o))

    row = lax.broadcasted_iota(jnp.int32, (256, 256), 0)
    col = lax.broadcasted_iota(jnp.int32, (256, 256), 1)
    chosen = col == lax.rem(row, 16) * 16 + lax.div(row, 16)
    perm[...] = jnp.where(chosen, 1.0, 0.0).astype(BF16)
    hit = jnp.sum(jnp.where(ids_ref[...] == z, rw_ref[...], 0.0), axis=0, keepdims=True)
    picked = jnp.sum(jnp.where(chosen, hit, 0.0), axis=1, keepdims=True)
    wrow[...] = jnp.broadcast_to(picked, (256, 128))
    decay = -jnp.exp(alog_ref[...])
    gate_z = jax.nn.silu(z_ref[...].astype(F32))
    wout_mate.wait_send()
    hid_mate.wait_send()

    others(16, t, lambda o: rcopy(proj, proj_in.at[o], PROJ, o, o, (e, o)).wait_recv())
    total = jnp.sum(proj_in[...].astype(F32), axis=0)

    step_size = jax.nn.softplus(
        jnp.dot(total[:, 0:512].astype(BF16), dtw[...], preferred_element_type=F32) + dtb_ref[...]
    )
    maps = total[:, 512:640].T
    b_map, c_map = maps[0:16, :], maps[16:32, :]
    driven = step_size * inputs
    for r in range(16):
        new = jnp.exp(step_size[r : r + 1, :] * decay) * ssm[r] + driven[r : r + 1, :] * b_map[:, r : r + 1]
        nssm_ref[r] = new
        readout[r : r + 1, :] = jnp.sum(new * c_map[:, r : r + 1], axis=0, keepdims=True)
    mix[e] = ((readout[...] + skip_ref[...] * inputs) * gate_z).astype(BF16)

    def mix_copy(o):
        return rcopy(mix.at[e], mix.at[e], MIX, o, z, at_z(o))

    def mix_from(o):
        return rcopy(mix.at[2 * o + c], mix.at[2 * o + c], MIX, o, o, at_z(o))

    def mix_to_mate(o):
        return rcopy(mix.at[2 * o + c], mix.at[2 * o + c], MIX_M, o, o, (mate, t))

    def mix_from_mate(o):
        return rcopy(mix.at[2 * o + m], mix.at[2 * o + m], MIX_M, o, o, (mate, t))

    others(8, z, lambda o: mix_copy(o).start())
    mix_to_mate(z).start()
    hid_from_mate.wait_recv()
    others(8, z, lambda o: hid_copy(o).start())
    hid_in[z] = hidh[z]
    others(8, z, lambda o: wout_from(o).wait_recv())

    def mix_pass(o):
        mix_from(o).wait_recv()
        mix_to_mate(o).start()

    others(8, z, mix_pass)
    mix_from_mate(z).wait_recv()
    others(8, z, lambda o: mix_from_mate(o).wait_recv())
    ordered = jnp.dot(perm[...], mix[...].reshape(256, 512), preferred_element_type=F32).astype(BF16)
    mixed = jnp.dot(ordered, ow[...].reshape(512, 256), preferred_element_type=F32)
    outb[...] = mixed.astype(BF16).reshape(16, 16, 256)

    def out_copy(o):
        return rcopy(outb.at[o], outr.at[t], OUTRED, o, t, (e, o))

    others(16, t, lambda o: out_copy(o).start())
    outr[t] = outb[t]
    down_mate(0).start()
    down_mate(1).start()
    others(16, t, lambda o: proj_copy(o).wait_send())
    others(8, z, lambda o: wout_copy(o).wait_send())
    others(8, z, lambda o: hid_copy(o).wait_send())
    others(8, z, lambda o: hid_from(o).wait_recv())
    others(8, z, lambda o: mix_copy(o).wait_send())
    mix_to_mate(z).wait_send()
    others(8, z, lambda o: mix_to_mate(o).wait_send())
    others(16, t, lambda o: rcopy(outb.at[o], outr.at[o], OUTRED, o, o, (e, o)).wait_recv())
    res[z] = (jnp.sum(outr[...].astype(F32), axis=0) + hid_in[...].reshape(16, 256)).astype(BF16)

    def res_copy(o):
        return rcopy(res.at[z], res.at[z], RESID, o, z, at_z(o))

    others(8, z, lambda o: res_copy(o).start())
    others(16, t, lambda o: out_copy(o).wait_send())
    others(8, z, lambda o: rcopy(res.at[o], res.at[o], RESID, o, o, at_z(o)).wait_recv())
    for b in range(8):
        gain = gain_ref[:, pl.ds(pl.multiple_of(c * 2048 + b * 256, 256), 256)]
        value = (res[b].astype(F32) * gain).astype(BF16)
        xn[2 * c + b // 4, y, x, :, (b % 4) * 256 : (b % 4 + 1) * 256] = value

    def rows1_x(o, frm):
        return rcopy(xn.at[q0, y, x], xn.at[q0, y, frm], ROWS1, o, frm, at_x(o))

    def rows1_y(o, frm):
        return rcopy(xn.at[q1, y, x], xn.at[q1, frm, x], ROWS1, 4 + o, 4 + frm, at_y(o))

    def rows2_y(o, frm):
        return rcopy(xn.at[q0, y], xn.at[q0, frm], ROWS2, o, frm, at_y(o))

    def rows2_x(o, frm):
        return rcopy(xn.at[q1, :, x], xn.at[q1, :, frm], ROWS2, 4 + o, 4 + frm, at_x(o))

    def pass_y(bx, o):
        return rcopy(xn.at[q0, y, bx], xn.at[q0, y, bx], ROWS2, o, y, at_y(o))

    def pass_x(by, o):
        return rcopy(xn.at[q1, by, x], xn.at[q1, by, x], ROWS2, 4 + o, 4 + x, at_x(o))

    def rows3_0(q, o):
        return rcopy(xn.at[q, o], xn.at[q, o], ROWS3, o, o, (mate, t))

    def rows3_1(q, o):
        return rcopy(xn.at[q, :, o], xn.at[q, :, o], ROWS3, 4 + o, 4 + o, (mate, t))

    others(4, x, lambda o: rows1_x(o, x).start())
    others(4, y, lambda o: rows1_y(o, y).start())
    others(4, y, lambda o: pass_y(x, o).start())
    others(4, x, lambda o: pass_x(y, o).start())
    squares = jnp.zeros((16, 256), F32)
    for b in range(8):
        piece = res[b].astype(F32)
        squares = squares + piece * piece
    sums = jnp.broadcast_to(jnp.sum(squares, axis=1, keepdims=True), (16, 128)).T
    stat[0] = jnp.zeros((1, 128), F32)
    stat[0, :, 0:16] = sums[0:1, :]
    stat_copy = rcopy(stat.at[0], stat.at[1], STAT, 0, 0, (mate, t))
    stat_copy.start()
    others(8, z, lambda o: res_copy(o).wait_send())
    stat_copy.wait()
    scales[t] = lax.rsqrt((stat[0] + stat[1]) * (1.0 / 4096) + 1e-5)

    def scale_copy(o):
        return rcopy(scales.at[t], scales.at[t], SCALE, o, t, (e, o))

    others(16, t, lambda o: scale_copy(o).start())
    place = lax.broadcasted_iota(jnp.int32, (16, 256), 0)
    for k in range(2):
        mine = place == 2 * z + k
        for b in range(8):
            line = jnp.sum(jnp.where(mine, res[b].astype(F32), 0.0), axis=0, keepdims=True)
            resrow[k, 2 * b : 2 * b + 1, :] = line[:, 0:128]
            resrow[k, 2 * b + 1 : 2 * b + 2, :] = line[:, 128:256]

    def line_pass(d, carry):
        bx, by = lax.rem(x + d, 4), lax.rem(y + d, 4)
        rows1_x(bx, bx).wait_recv()
        others(4, y, lambda o: pass_y(bx, o).start())
        rows1_y(by, by).wait_recv()
        others(4, x, lambda o: pass_x(by, o).start())
        return carry

    lax.fori_loop(1, 4, line_pass, 0)
    rows3_0(q0, y).start()
    rows3_1(q1, x).start()
    for copy in weights:
        copy.wait()
    for s in range(2):
        down_mate(s).wait()
    others(4, x, lambda o: rows1_x(o, x).wait_send())
    others(4, y, lambda o: rows1_y(o, y).wait_send())

    others(16, t, lambda o: rcopy(scales.at[o], scales.at[o], SCALE, o, o, (e, o)).wait_recv())
    lane = lax.broadcasted_iota(jnp.int32, (16, 16, 128), 2)
    slot = lax.broadcasted_iota(jnp.int32, (16, 16, 128), 1)
    picked = jnp.where(lane == slot, jnp.broadcast_to(scales[...], (16, 16, 128)), 0.0).reshape(256, 128)
    scale = jnp.broadcast_to(jnp.sum(picked, axis=1, keepdims=True), (256, 384))

    def forward(d, carry):
        oy, ox = lax.rem(y + d, 4), lax.rem(x + d, 4)
        rows2_y(oy, oy).wait_recv()
        rows3_0(q0, oy).start()
        rows2_x(ox, ox).wait_recv()
        rows3_1(q1, ox).start()
        return carry

    lax.fori_loop(1, 4, forward, 0)

    acc_g[...] = jnp.zeros((256, 384), F32)
    acc_u[...] = jnp.zeros((256, 384), F32)

    def project(q):
        rows = xn[q].reshape(256, 1024)
        acc_g[...] += jnp.dot(rows, wg[q], preferred_element_type=F32)
        acc_u[...] += jnp.dot(rows, wu[q], preferred_element_type=F32)

    def project_half(first):
        def step(s, carry):
            project(first + s)
            return carry
        lax.fori_loop(0, 2, step, 0)

    project_half(q0)

    def mate_rows(o, carry):
        rows3_0(p0, o).wait_recv()
        rows3_1(p0 + 1, o).wait_recv()
        return carry

    lax.fori_loop(0, 4, mate_rows, 0)
    project_half(p0)
    weight = jnp.concatenate([wrow[...]] * 3, axis=1)
    actw[...] = (jax.nn.silu(acc_g[...] * scale) * (acc_u[...] * scale) * weight).astype(BF16)

    act_copy = rcopy(actw, act_mate, ACT, 0, 0, (mate, t))
    act_copy.start()

    def red1_x(o, frm):
        return rcopy(own.at[0, :, o], red1.at[0, frm], RED1, o, frm, at_x(o))

    def red1_y(o, frm):
        return rcopy(own.at[1, o], red1.at[1, frm], RED1, 4 + o, 4 + frm, at_y(o))

    value = jnp.dot(actw[...], wd[0], preferred_element_type=F32)
    act_copy.wait()
    value = value + jnp.dot(act_mate[...], wd_mate[0], preferred_element_type=F32)
    own[0] = value.astype(BF16).reshape(4, 4, 16, 1024)
    others(4, x, lambda o: red1_x(o, x).start())
    value = jnp.dot(actw[...], wd[1], preferred_element_type=F32)
    value = value + jnp.dot(act_mate[...], wd_mate[1], preferred_element_type=F32)
    own[1] = value.astype(BF16).reshape(4, 4, 16, 1024)
    others(4, y, lambda o: red1_y(o, y).start())

    others(16, t, lambda o: scale_copy(o).wait_send())
    others(4, y, lambda o: rows2_y(o, y).wait_send())
    others(4, x, lambda o: rows2_x(o, x).wait_send())

    def rows3_sent(o, carry):
        rows3_0(q0, o).wait_send()
        rows3_1(q1, o).wait_send()
        return carry

    lax.fori_loop(0, 4, rows3_sent, 0)

    def red2_y(o, frm):
        return rcopy(tsum.at[0, o], red2.at[0, frm], RED2, o, frm, at_y(o))

    def red2_x(o, frm):
        return rcopy(tsum.at[1, o], red2.at[1, frm], RED2, 4 + o, 4 + frm, at_x(o))

    others(4, x, lambda o: red1_x(o, o).wait_recv())
    value = own[0, :, x].astype(F32)
    for d in range(1, 4):
        value = value + red1[0, lax.rem(x + d, 4)].astype(F32)
    tsum[0] = value.astype(BF16)
    others(4, y, lambda o: red2_y(o, y).start())
    others(4, y, lambda o: red1_y(o, o).wait_recv())
    value = own[1, y].astype(F32)
    for d in range(1, 4):
        value = value + red1[1, lax.rem(y + d, 4)].astype(F32)
    tsum[1] = value.astype(BF16)
    others(4, x, lambda o: red2_x(o, x).start())
    others(4, x, lambda o: red1_x(o, x).wait_send())
    others(4, y, lambda o: red1_y(o, y).wait_send())

    others(4, y, lambda o: red2_y(o, o).wait_recv())
    first = tsum[0, y].astype(F32)
    for d in range(1, 4):
        first = first + red2[0, lax.rem(y + d, 4)].astype(F32)
    others(4, x, lambda o: red2_x(o, o).wait_recv())
    second = tsum[1, x].astype(F32)
    for d in range(1, 4):
        second = second + red2[1, lax.rem(x + d, 4)].astype(F32)

    for k in range(8):
        vrow[:, k, :] = first[:, 128 * k : 128 * (k + 1)]
        vrow[:, 8 + k, :] = second[:, 128 * k : 128 * (k + 1)]
    vrow[pl.ds(2 * z, 2)] += resrow[...]
    vsend[...] = vrow[...].astype(BF16)

    def final_copy(o):
        return rcopy(vsend.at[o], final_in.at[e], FINAL, o, e, (o, t))

    others(16, e, lambda o: final_copy(o).start())
    final_in[e] = vsend[e]
    others(4, y, lambda o: red2_y(o, y).wait_send())
    others(4, x, lambda o: red2_x(o, x).wait_send())
    others(16, e, lambda o: rcopy(vsend.at[o], final_in.at[o], FINAL, o, o, (o, t)).wait_recv())
    for k in range(2):
        value = final_in[k].astype(F32)
        for b in range(1, 8):
            value = value + final_in[2 * b + k].astype(F32)
        for b in range(16):
            out_ref[:, 2048 * k + 128 * b : 2048 * k + 128 * (b + 1)] = value[b : b + 1, :]
    others(16, e, lambda o: final_copy(o).wait_send())


def finish_kernel(row, ncs, nssm, row_out, ncs_out, nssm_out, sem):
    copies = [pltpu.make_async_copy(nssm, nssm_out, sem.at[0]), pltpu.make_async_copy(ncs, ncs_out, sem.at[1])]
    for copy in copies:
        copy.start()
    row_out[...] = row[...].astype(BF16)
    for copy in copies:
        copy.wait()


def local(
    hidden_in,
    x_stream,
    z_stream,
    conv_state,
    ssm_state,
    conv_weight,
    conv_bias,
    x_weight,
    dt_weight,
    dt_bias,
    a_log,
    skip_gain,
    out_weight,
    norm_gain,
    route_ids,
    route_weights,
    gate_proj,
    up_proj,
    down_proj,
):
    vmem = pl.BlockSpec(memory_space=pltpu.VMEM)
    hbm = pl.BlockSpec(memory_space=pltpu.HBM)
    row, new_conv_state, new_ssm_state = pl.pallas_call(
        layer_kernel,
        out_shape=(
            pltpu.VMEM((1, 4096), F32),
            pltpu.VMEM((3, 16, 512), BF16),
            pltpu.VMEM((16, 16, 512), F32),
        ),
        in_specs=[hbm] * 19,
        out_specs=(vmem, vmem, vmem),
        scratch_shapes=[
            pltpu.VMEM((16, 512), BF16),
            pltpu.VMEM((16, 512), BF16),
            pltpu.VMEM((3, 16, 512), BF16),
            pltpu.VMEM((4, 512), BF16),
            pltpu.VMEM((1, 512), F32),
            pltpu.VMEM((544, 512), BF16),
            pltpu.VMEM((1, 512), F32),
            pltpu.VMEM((16, 512), F32),
            pltpu.VMEM((1, 512), F32),
            pltpu.VMEM((1, 4096), F32),
            pltpu.VMEM((2, 256), jnp.int32),
            pltpu.VMEM((2, 256), F32),
            pltpu.VMEM((1, 4096), BF16),
            pltpu.VMEM((512, 512), BF16),
            pltpu.VMEM((16, 16, 512), F32),
            pltpu.VMEM((4, 1024, 384), BF16),
            pltpu.VMEM((4, 1024, 384), BF16),
            pltpu.VMEM((2, 384, 1024), BF16),
            pltpu.VMEM((2, 384, 1024), BF16),
            pltpu.VMEM((2, 32, 2048), BF16),
            pltpu.VMEM((8, 2, 32, 256), BF16),
            pltpu.VMEM((16, 640), BF16),
            pltpu.VMEM((16, 16, 640), BF16),
            pltpu.VMEM((16, 1, 256), F32),
            pltpu.VMEM((8, 2, 1, 256), F32),
            pltpu.VMEM((8, 2, 1, 256), F32),
            pltpu.VMEM((16, 512), F32),
            pltpu.VMEM((16, 16, 512), BF16),
            pltpu.VMEM((16, 16, 256), BF16),
            pltpu.VMEM((16, 16, 256), BF16),
            pltpu.VMEM((8, 16, 256), BF16),
            pltpu.VMEM((2, 1, 128), F32),
            pltpu.VMEM((16, 1, 128), F32),
            pltpu.VMEM((2, 16, 128), F32),
            pltpu.VMEM((4, 4, 4, 16, 1024), BF16),
            pltpu.VMEM((256, 384), F32),
            pltpu.VMEM((256, 384), F32),
            pltpu.VMEM((256, 384), BF16),
            pltpu.VMEM((256, 384), BF16),
            pltpu.VMEM((256, 128), F32),
            pltpu.VMEM((256, 256), BF16),
            pltpu.VMEM((2, 4, 4, 16, 1024), BF16),
            pltpu.VMEM((2, 4, 4, 16, 1024), BF16),
            pltpu.VMEM((2, 4, 16, 1024), BF16),
            pltpu.VMEM((2, 4, 16, 1024), BF16),
            pltpu.VMEM((16, 16, 128), F32),
            pltpu.VMEM((16, 16, 128), BF16),
            pltpu.VMEM((16, 16, 128), BF16),
            pltpu.SemaphoreType.DMA((19, 16)),
            pltpu.SemaphoreType.DMA((19, 16)),
            pltpu.SemaphoreType.DMA((32,)),
        ],
        compiler_params=pltpu.CompilerParams(
            collective_id=0, has_side_effects=True, vmem_limit_bytes=48 * 1024 * 1024
        ),
        name="layer",
    )(*(
        pltpu.with_memory_space_constraint(operand, pltpu.HBM) for operand in (
            x_stream, z_stream, conv_state.transpose(1, 0, 2), conv_weight, conv_bias[None], x_weight.T,
            dt_bias[None], a_log, skip_gain[None], norm_gain[None], route_ids.T, route_weights.T, hidden_in,
            dt_weight, ssm_state, out_weight, gate_proj, up_proj, down_proj,
        )
    ))
    row, new_conv_state, new_ssm_state = pl.pallas_call(
        finish_kernel,
        out_shape=(
            jax.ShapeDtypeStruct((1, 4096), BF16),
            jax.ShapeDtypeStruct((3, 16, 512), BF16),
            jax.ShapeDtypeStruct((16, 16, 512), F32),
        ),
        in_specs=[vmem] * 3,
        out_specs=(vmem, hbm, hbm),
        scratch_shapes=[pltpu.SemaphoreType.DMA((2,))],
        compiler_params=pltpu.CompilerParams(vmem_limit_bytes=48 * 1024 * 1024),
        name="finish",
    )(row, new_conv_state, new_ssm_state)
    return (row, new_conv_state.transpose(1, 0, 2), new_ssm_state)


def solution(mesh):
    return jax.shard_map(
        local,
        mesh=mesh,
        in_specs=(
            P(("expert", "tensor"), None),
            P("expert", "tensor"),
            P("expert", "tensor"),
            P("expert", None, "tensor"),
            P("expert", None, "tensor"),
            P(None, "tensor"),
            P("tensor"),
            P("tensor", None),
            P(None, "tensor"),
            P("tensor"),
            P(None, "tensor"),
            P("tensor"),
            P("tensor", "expert", None),
            P(),
            P(),
            P(),
            P("expert", None, "tensor"),
            P("expert", None, "tensor"),
            P("expert", "tensor", None),
        ),
        out_specs=(
            P(("expert", "tensor"), None),
            P("expert", None, "tensor"),
            P("expert", None, "tensor"),
        ),
        check_vma=False,
    )
```

```python
import jax
import jax.numpy as jnp
from jax import lax
from jax.experimental import pallas as pl
from jax.experimental.pallas import tpu as pltpu
from jax.sharding import PartitionSpec as P

F32 = jnp.float32
BF16 = jnp.bfloat16
MESH = pl.DeviceIdType.MESH

(
    PROJ, WOUT_M, WOUT, HID_M, HID, DOWN_M, MIX, MIX_M, OUTRED, RESID, STAT, SCALE,
    ROWS1, ROWS2, ROWS3, ACT, RED1, RED2, FINAL,
) = range(19)


def layer_kernel(
    x_hbm, z_hbm, cs_hbm, cw_hbm, cb_hbm, xw_hbm, dtb_hbm, alog_hbm, skip_hbm, gain_hbm, ids_hbm, rw_hbm, hid_hbm,
    dtw_hbm, ssm_hbm, ow_hbm, gate_hbm, up_hbm, down_hbm,
    out_ref, ncs_ref, nssm_ref,
    x_ref, z_ref, cs_ref, cw_ref, cb_ref, xw_ref, dtb_ref, alog_ref, skip_ref, gain_ref, ids_ref, rw_ref, hid_ref,
    dtw, ssm, wg, wu, wd, wd_mate, owh, ow,
    proj, proj_in, hid_out, hidh, hid_in, readout, mix, outb, outr, res, stat, scales, resrow, xn, acc_g, acc_u,
    actw, act_mate, wrow, perm, own, red1, tsum, red2, vrow, vsend, final_in,
    ssem, rsem, lsem,
):
    e = lax.axis_index("expert")
    t = lax.axis_index("tensor")
    y, x = lax.div(t, 4), lax.rem(t, 4)
    z, c = lax.div(e, 2), lax.rem(e, 2)
    m = 1 - c
    mate = 2 * z + m
    q0, q1 = 2 * c, 2 * c + 1
    p0 = 2 * m

    def rcopy(src, dst, phase, to, frm, device):
        return pltpu.make_async_remote_copy(
            src_ref=src, dst_ref=dst, send_sem=ssem.at[phase, to], recv_sem=rsem.at[phase, frm],
            device_id=device, device_id_type=MESH,
        )

    def others(n, me, body):
        def step(d, carry):
            body(lax.rem(me + (5 * d if n == 16 else 3 * d if n == 8 else 3 - d + lax.div(d, 3) * 3), n))
            return carry
        lax.fori_loop(1, n, step, 0)

    def at_z(o):
        return (2 * o + c, t)

    def at_x(o):
        return (e, y * 4 + o)

    def at_y(o):
        return (e, o * 4 + x)

    def half(which):
        return pl.ds(pl.multiple_of(which * 2048, 2048), 2048)

    def lcopy(src, dst, i):
        return pltpu.make_async_copy(src, dst, lsem.at[i])

    early = [
        lcopy(src, dst, i) for i, (src, dst) in enumerate((
            (x_hbm, x_ref), (cs_hbm, cs_ref), (cw_hbm, cw_ref), (cb_hbm, cb_ref),
        ))
    ]
    later = [
        lcopy(src, dst, 5 + i) for i, (src, dst) in enumerate((
            (hid_hbm, hid_ref), (dtw_hbm, dtw), (ssm_hbm, ssm), (ids_hbm, ids_ref), (rw_hbm, rw_ref),
            (z_hbm, z_ref), (dtb_hbm, dtb_ref), (alog_hbm, alog_ref), (skip_hbm, skip_ref), (gain_hbm, gain_ref),
        ))
    ]
    weights = []
    for q in range(4):
        weights.append(lcopy(gate_hbm.at[0, pl.ds(q * 1024, 1024), :], wg.at[q], 16 + q))
        weights.append(lcopy(up_hbm.at[0, pl.ds(q * 1024, 1024), :], wu.at[q], 20 + q))

    def down_cols(which, s):
        return down_hbm.at[0, :, pl.ds(pl.multiple_of(which * 2048 + s * 1024, 1024), 1024)]

    for s in range(2):
        weights.append(lcopy(down_cols(c, s), wd.at[s], 24 + s))
    for k in range(4):
        part = pl.ds(k * 128, 128 if k < 3 else 160)
        early.append(lcopy(xw_hbm.at[part], xw_ref.at[part], 28 + k))
    own_weight = lcopy(ow_hbm.at[0, :, half(c)], owh.at[c], 15)
    for copy in early:
        copy.start()
    own_weight.start()

    def greet(device):
        pl.semaphore_signal(bar, inc=1, device_id=device, device_id_type=MESH)

    bar = pltpu.get_barrier_semaphore()
    others(16, t, lambda o: greet((e, o)))
    others(8, z, lambda o: greet(at_z(o)))
    greet((mate, t))

    for copy in early:
        copy.wait()
    state = cs_ref[...].astype(F32)
    taps = cw_ref[...].astype(F32)
    newest = x_ref[...].astype(F32)
    window = [state[0], state[1], state[2], newest]
    conv_sum = sum(window[k] * taps[k : k + 1, :] for k in range(4)) + cb_ref[...]
    conv_out = jax.nn.silu(conv_sum).astype(BF16)
    inputs = conv_out.astype(F32)
    part = lax.dot_general(
        conv_out, xw_ref[...], (((1,), (1,)), ((), ())), preferred_element_type=F32
    )
    proj[...] = jnp.zeros((16, 640), BF16)
    proj[:, 0:544] = part.astype(BF16)

    pl.semaphore_wait(bar, 23)

    def wout_copy(o):
        cols = pl.ds(pl.multiple_of(o * 256, 256), 256)
        return rcopy(owh.at[:, :, cols], ow.at[z], WOUT, o, z, at_z(o))

    def wout_from(o):
        return rcopy(ow.at[o], ow.at[o], WOUT, o, o, at_z(o))

    def proj_copy(o):
        return rcopy(proj, proj_in.at[t], PROJ, o, t, (e, o))

    wout_mate = rcopy(ow_hbm.at[0, :, half(m)], owh.at[c], WOUT_M, 0, 0, (mate, t))
    wout_from_mate = rcopy(ow_hbm.at[0, :, half(m)], owh.at[m], WOUT_M, 0, 0, (mate, t))
    wout_mate.start()
    others(16, t, lambda o: proj_copy(o).start())
    proj_in[t] = proj[...]
    wout_from_mate.wait_recv()
    own_weight.wait()
    others(8, z, lambda o: wout_copy(o).start())

    hid_mate = rcopy(hid_out.at[pl.ds(8 * m, 8)], hidh.at[:, c], HID_M, 0, 0, (mate, t))
    hid_from_mate = rcopy(hid_out.at[pl.ds(8 * m, 8)], hidh.at[:, m], HID_M, 0, 0, (mate, t))

    def down_mate(s):
        return rcopy(down_cols(m, s), wd_mate.at[s], DOWN_M, s, s, (mate, t))

    for copy in later:
        copy.start()
    for copy in weights:
        copy.start()
    for copy in later:
        copy.wait()
    hidden = hid_ref[...].astype(F32)
    for k in range(16):
        hid_out[k] = hidden[:, 256 * k : 256 * (k + 1)]
    hid_mate.start()
    hidh[:, c] = hid_out[pl.ds(8 * c, 8)]
    ncs_ref[0] = cs_ref[1]
    ncs_ref[1] = cs_ref[2]
    ncs_ref[2] = x_ref[...]

    ow[z] = owh[:, :, pl.ds(pl.multiple_of(z * 256, 256), 256)]

    def hid_copy(o):
        return rcopy(hidh.at[o], hid_in.at[z], HID, o, z, at_z(o))

    def hid_from(o):
        return rcopy(hidh.at[o], hid_in.at[o], HID, o, o, at_z(o))

    row = lax.broadcasted_iota(jnp.int32, (256, 256), 0)
    col = lax.broadcasted_iota(jnp.int32, (256, 256), 1)
    chosen = col == lax.rem(row, 16) * 16 + lax.div(row, 16)
    perm[...] = jnp.where(chosen, 1.0, 0.0).astype(BF16)
    hit = jnp.sum(jnp.where(ids_ref[...] == z, rw_ref[...], 0.0), axis=0, keepdims=True)
    picked = jnp.sum(jnp.where(chosen, hit, 0.0), axis=1, keepdims=True)
    wrow[...] = jnp.broadcast_to(picked, (256, 128))
    decay = -jnp.exp(alog_ref[...])
    gate_z = jax.nn.silu(z_ref[...].astype(F32))
    wout_mate.wait_send()
    hid_mate.wait_send()

    others(16, t, lambda o: rcopy(proj, proj_in.at[o], PROJ, o, o, (e, o)).wait_recv())
    total = jnp.sum(proj_in[...].astype(F32), axis=0)

    step_size = jax.nn.softplus(
        jnp.dot(total[:, 0:512].astype(BF16), dtw[...], preferred_element_type=F32) + dtb_ref[...]
    )
    maps = total[:, 512:640].T
    b_map, c_map = maps[0:16, :], maps[16:32, :]
    driven = step_size * inputs
    for r in range(16):
        new = jnp.exp(step_size[r : r + 1, :] * decay) * ssm[r] + driven[r : r + 1, :] * b_map[:, r : r + 1]
        nssm_ref[r] = new
        readout[r : r + 1, :] = jnp.sum(new * c_map[:, r : r + 1], axis=0, keepdims=True)
    mix[e] = ((readout[...] + skip_ref[...] * inputs) * gate_z).astype(BF16)

    def mix_copy(o):
        return rcopy(mix.at[e], mix.at[e], MIX, o, z, at_z(o))

    def mix_from(o):
        return rcopy(mix.at[2 * o + c], mix.at[2 * o + c], MIX, o, o, at_z(o))

    def mix_to_mate(o):
        return rcopy(mix.at[2 * o + c], mix.at[2 * o + c], MIX_M, o, o, (mate, t))

    def mix_from_mate(o):
        return rcopy(mix.at[2 * o + m], mix.at[2 * o + m], MIX_M, o, o, (mate, t))

    others(8, z, lambda o: mix_copy(o).start())
    mix_to_mate(z).start()
    hid_from_mate.wait_recv()
    others(8, z, lambda o: hid_copy(o).start())
    hid_in[z] = hidh[z]
    others(8, z, lambda o: wout_from(o).wait_recv())

    def mix_pass(o):
        mix_from(o).wait_recv()
        mix_to_mate(o).start()

    others(8, z, mix_pass)
    mix_from_mate(z).wait_recv()
    others(8, z, lambda o: mix_from_mate(o).wait_recv())
    ordered = jnp.dot(perm[...], mix[...].reshape(256, 512), preferred_element_type=F32).astype(BF16)
    mixed = jnp.dot(ordered, ow[...].reshape(512, 256), preferred_element_type=F32)
    outb[...] = mixed.astype(BF16).reshape(16, 16, 256)

    def out_copy(o):
        return rcopy(outb.at[o], outr.at[t], OUTRED, o, t, (e, o))

    others(16, t, lambda o: out_copy(o).start())
    outr[t] = outb[t]
    down_mate(0).start()
    down_mate(1).start()
    others(16, t, lambda o: proj_copy(o).wait_send())
    others(8, z, lambda o: wout_copy(o).wait_send())
    others(8, z, lambda o: hid_copy(o).wait_send())
    others(8, z, lambda o: hid_from(o).wait_recv())
    others(8, z, lambda o: mix_copy(o).wait_send())
    mix_to_mate(z).wait_send()
    others(8, z, lambda o: mix_to_mate(o).wait_send())
    others(16, t, lambda o: rcopy(outb.at[o], outr.at[o], OUTRED, o, o, (e, o)).wait_recv())
    res[z] = (jnp.sum(outr[...].astype(F32), axis=0) + hid_in[...].reshape(16, 256)).astype(BF16)

    def res_copy(o):
        return rcopy(res.at[z], res.at[z], RESID, o, z, at_z(o))

    others(8, z, lambda o: res_copy(o).start())
    others(16, t, lambda o: out_copy(o).wait_send())
    others(8, z, lambda o: rcopy(res.at[o], res.at[o], RESID, o, o, at_z(o)).wait_recv())
    for b in range(8):
        gain = gain_ref[:, pl.ds(pl.multiple_of(c * 2048 + b * 256, 256), 256)]
        value = (res[b].astype(F32) * gain).astype(BF16)
        xn[2 * c + b // 4, y, x, :, (b % 4) * 256 : (b % 4 + 1) * 256] = value

    def rows1_x(o, frm):
        return rcopy(xn.at[q0, y, x], xn.at[q0, y, frm], ROWS1, o, frm, at_x(o))

    def rows1_y(o, frm):
        return rcopy(xn.at[q1, y, x], xn.at[q1, frm, x], ROWS1, 4 + o, 4 + frm, at_y(o))

    def rows2_y(o, frm):
        return rcopy(xn.at[q0, y], xn.at[q0, frm], ROWS2, o, frm, at_y(o))

    def rows2_x(o, frm):
        return rcopy(xn.at[q1, :, x], xn.at[q1, :, frm], ROWS2, 4 + o, 4 + frm, at_x(o))

    def pass_y(bx, o):
        return rcopy(xn.at[q0, y, bx], xn.at[q0, y, bx], ROWS2, o, y, at_y(o))

    def pass_x(by, o):
        return rcopy(xn.at[q1, by, x], xn.at[q1, by, x], ROWS2, 4 + o, 4 + x, at_x(o))

    def rows3_0(q, o):
        return rcopy(xn.at[q, o], xn.at[q, o], ROWS3, o, o, (mate, t))

    def rows3_1(q, o):
        return rcopy(xn.at[q, :, o], xn.at[q, :, o], ROWS3, 4 + o, 4 + o, (mate, t))

    others(4, x, lambda o: rows1_x(o, x).start())
    others(4, y, lambda o: rows1_y(o, y).start())
    others(4, y, lambda o: pass_y(x, o).start())
    others(4, x, lambda o: pass_x(y, o).start())
    squares = jnp.zeros((16, 256), F32)
    for b in range(8):
        piece = res[b].astype(F32)
        squares = squares + piece * piece
    sums = jnp.broadcast_to(jnp.sum(squares, axis=1, keepdims=True), (16, 128)).T
    stat[0] = jnp.zeros((1, 128), F32)
    stat[0, :, 0:16] = sums[0:1, :]
    stat_copy = rcopy(stat.at[0], stat.at[1], STAT, 0, 0, (mate, t))
    stat_copy.start()
    others(8, z, lambda o: res_copy(o).wait_send())
    stat_copy.wait()
    scales[t] = lax.rsqrt((stat[0] + stat[1]) * (1.0 / 4096) + 1e-5)

    def scale_copy(o):
        return rcopy(scales.at[t], scales.at[t], SCALE, o, t, (e, o))

    others(16, t, lambda o: scale_copy(o).start())
    place = lax.broadcasted_iota(jnp.int32, (16, 256), 0)
    for k in range(2):
        mine = place == 2 * z + k
        for b in range(8):
            line = jnp.sum(jnp.where(mine, res[b].astype(F32), 0.0), axis=0, keepdims=True)
            resrow[k, 2 * b : 2 * b + 1, :] = line[:, 0:128]
            resrow[k, 2 * b + 1 : 2 * b + 2, :] = line[:, 128:256]

    def line_pass(d, carry):
        bx, by = lax.rem(x + d, 4), lax.rem(y + d, 4)
        rows1_x(bx, bx).wait_recv()
        others(4, y, lambda o: pass_y(bx, o).start())
        rows1_y(by, by).wait_recv()
        others(4, x, lambda o: pass_x(by, o).start())
        return carry

    lax.fori_loop(1, 4, line_pass, 0)
    rows3_0(q0, y).start()
    rows3_1(q1, x).start()
    for copy in weights:
        copy.wait()
    for s in range(2):
        down_mate(s).wait()
    others(4, x, lambda o: rows1_x(o, x).wait_send())
    others(4, y, lambda o: rows1_y(o, y).wait_send())

    others(16, t, lambda o: rcopy(scales.at[o], scales.at[o], SCALE, o, o, (e, o)).wait_recv())
    lane = lax.broadcasted_iota(jnp.int32, (16, 16, 128), 2)
    slot = lax.broadcasted_iota(jnp.int32, (16, 16, 128), 1)
    picked = jnp.where(lane == slot, jnp.broadcast_to(scales[...], (16, 16, 128)), 0.0).reshape(256, 128)
    scale = jnp.broadcast_to(jnp.sum(picked, axis=1, keepdims=True), (256, 384))

    def forward(d, carry):
        oy, ox = lax.rem(y + d, 4), lax.rem(x + d, 4)
        rows2_y(oy, oy).wait_recv()
        rows3_0(q0, oy).start()
        rows2_x(ox, ox).wait_recv()
        rows3_1(q1, ox).start()
        return carry

    lax.fori_loop(1, 4, forward, 0)

    acc_g[...] = jnp.zeros((256, 384), F32)
    acc_u[...] = jnp.zeros((256, 384), F32)

    def project(q):
        rows = xn[q].reshape(256, 1024)
        acc_g[...] += jnp.dot(rows, wg[q], preferred_element_type=F32)
        acc_u[...] += jnp.dot(rows, wu[q], preferred_element_type=F32)

    def project_half(first):
        def step(s, carry):
            project(first + s)
            return carry
        lax.fori_loop(0, 2, step, 0)

    project_half(q0)

    def mate_rows(o, carry):
        rows3_0(p0, o).wait_recv()
        rows3_1(p0 + 1, o).wait_recv()
        return carry

    lax.fori_loop(0, 4, mate_rows, 0)
    project_half(p0)
    weight = jnp.concatenate([wrow[...]] * 3, axis=1)
    actw[...] = (jax.nn.silu(acc_g[...] * scale) * (acc_u[...] * scale) * weight).astype(BF16)

    act_copy = rcopy(actw, act_mate, ACT, 0, 0, (mate, t))
    act_copy.start()

    def red1_copy(s, h, o, frm):
        if s == 0:
            return rcopy(own.at[0, h, :, o], red1.at[0, h, frm], RED1, 4 * h + o, 4 * h + frm, at_x(o))
        return rcopy(own.at[1, h, o], red1.at[1, h, frm], RED1, 8 + 4 * h + o, 8 + 4 * h + frm, at_y(o))

    def red2_copy(s, h, o, frm):
        if s == 0:
            return rcopy(tsum.at[0, h, o], red2.at[0, h, frm], RED2, 4 * h + o, 4 * h + frm, at_y(o))
        return rcopy(tsum.at[1, h, o], red2.at[1, h, frm], RED2, 8 + 4 * h + o, 8 + 4 * h + frm, at_x(o))

    one, two = (x, y), (y, x)

    def down(s, h, act, weight):
        return jnp.dot(act[...], weight[s, :, 512 * h : 512 * (h + 1)], preferred_element_type=F32)

    parts = [(0, 0), (1, 0), (0, 1), (1, 1)]
    for s, h in parts:
        value = down(s, h, actw, wd)
        if (s, h) == (0, 0):
            act_copy.wait()
        value = value + down(s, h, act_mate, wd_mate)
        own[s, h] = value.astype(BF16).reshape(4, 4, 16, 512)
        others(4, one[s], lambda o: red1_copy(s, h, o, one[s]).start())

    others(16, t, lambda o: scale_copy(o).wait_send())
    others(4, y, lambda o: rows2_y(o, y).wait_send())
    others(4, x, lambda o: rows2_x(o, x).wait_send())

    def rows3_sent(o, carry):
        rows3_0(q0, o).wait_send()
        rows3_1(q1, o).wait_send()
        return carry

    lax.fori_loop(0, 4, rows3_sent, 0)

    for s, h in parts:
        others(4, one[s], lambda o: red1_copy(s, h, o, o).wait_recv())
        value = (own[0, h, :, x] if s == 0 else own[1, h, y]).astype(F32)
        for d in range(1, 4):
            value = value + red1[s, h, lax.rem(one[s] + d, 4)].astype(F32)
        tsum[s, h] = value.astype(BF16)
        others(4, two[s], lambda o: red2_copy(s, h, o, two[s]).start())
    for s, h in parts:
        others(4, one[s], lambda o: red1_copy(s, h, o, one[s]).wait_send())

    for s, h in parts:
        others(4, two[s], lambda o: red2_copy(s, h, o, o).wait_recv())
        value = tsum[s, h, two[s]].astype(F32)
        for d in range(1, 4):
            value = value + red2[s, h, lax.rem(two[s] + d, 4)].astype(F32)
        for k in range(4):
            vrow[:, 8 * s + 4 * h + k, :] = value[:, 128 * k : 128 * (k + 1)]

    vrow[pl.ds(2 * z, 2)] += resrow[...]
    vsend[...] = vrow[...].astype(BF16)

    def final_copy(o):
        return rcopy(vsend.at[o], final_in.at[e], FINAL, o, e, (o, t))

    others(16, e, lambda o: final_copy(o).start())
    final_in[e] = vsend[e]
    for s, h in parts:
        others(4, two[s], lambda o: red2_copy(s, h, o, two[s]).wait_send())
    others(16, e, lambda o: rcopy(vsend.at[o], final_in.at[o], FINAL, o, o, (o, t)).wait_recv())
    for k in range(2):
        value = final_in[k].astype(F32)
        for b in range(1, 8):
            value = value + final_in[2 * b + k].astype(F32)
        for b in range(16):
            out_ref[:, 2048 * k + 128 * b : 2048 * k + 128 * (b + 1)] = value[b : b + 1, :]
    others(16, e, lambda o: final_copy(o).wait_send())


def finish_kernel(row, ncs, nssm, row_out, ncs_out, nssm_out, sem):
    copies = [
        pltpu.make_async_copy(nssm.at[pl.ds(4 * k, 4)], nssm_out.at[pl.ds(4 * k, 4)], sem.at[k]) for k in range(4)
    ]
    copies.append(pltpu.make_async_copy(ncs, ncs_out, sem.at[4]))
    for copy in copies:
        copy.start()
    row_out[...] = row[...].astype(BF16)
    for copy in copies:
        copy.wait()


def local(
    hidden_in,
    x_stream,
    z_stream,
    conv_state,
    ssm_state,
    conv_weight,
    conv_bias,
    x_weight,
    dt_weight,
    dt_bias,
    a_log,
    skip_gain,
    out_weight,
    norm_gain,
    route_ids,
    route_weights,
    gate_proj,
    up_proj,
    down_proj,
):
    vmem = pl.BlockSpec(memory_space=pltpu.VMEM)
    hbm = pl.BlockSpec(memory_space=pltpu.HBM)
    row, new_conv_state, new_ssm_state = pl.pallas_call(
        layer_kernel,
        out_shape=(
            pltpu.VMEM((1, 4096), F32),
            pltpu.VMEM((3, 16, 512), BF16),
            pltpu.VMEM((16, 16, 512), F32),
        ),
        in_specs=[hbm] * 19,
        out_specs=(vmem, vmem, vmem),
        scratch_shapes=[
            pltpu.VMEM((16, 512), BF16),
            pltpu.VMEM((16, 512), BF16),
            pltpu.VMEM((3, 16, 512), BF16),
            pltpu.VMEM((4, 512), BF16),
            pltpu.VMEM((1, 512), F32),
            pltpu.VMEM((544, 512), BF16),
            pltpu.VMEM((1, 512), F32),
            pltpu.VMEM((16, 512), F32),
            pltpu.VMEM((1, 512), F32),
            pltpu.VMEM((1, 4096), F32),
            pltpu.VMEM((2, 256), jnp.int32),
            pltpu.VMEM((2, 256), F32),
            pltpu.VMEM((1, 4096), BF16),
            pltpu.VMEM((512, 512), BF16),
            pltpu.VMEM((16, 16, 512), F32),
            pltpu.VMEM((4, 1024, 384), BF16),
            pltpu.VMEM((4, 1024, 384), BF16),
            pltpu.VMEM((2, 384, 1024), BF16),
            pltpu.VMEM((2, 384, 1024), BF16),
            pltpu.VMEM((2, 32, 2048), BF16),
            pltpu.VMEM((8, 2, 32, 256), BF16),
            pltpu.VMEM((16, 640), BF16),
            pltpu.VMEM((16, 16, 640), BF16),
            pltpu.VMEM((16, 1, 256), F32),
            pltpu.VMEM((8, 2, 1, 256), F32),
            pltpu.VMEM((8, 2, 1, 256), F32),
            pltpu.VMEM((16, 512), F32),
            pltpu.VMEM((16, 16, 512), BF16),
            pltpu.VMEM((16, 16, 256), BF16),
            pltpu.VMEM((16, 16, 256), BF16),
            pltpu.VMEM((8, 16, 256), BF16),
            pltpu.VMEM((2, 1, 128), F32),
            pltpu.VMEM((16, 1, 128), F32),
            pltpu.VMEM((2, 16, 128), F32),
            pltpu.VMEM((4, 4, 4, 16, 1024), BF16),
            pltpu.VMEM((256, 384), F32),
            pltpu.VMEM((256, 384), F32),
            pltpu.VMEM((256, 384), BF16),
            pltpu.VMEM((256, 384), BF16),
            pltpu.VMEM((256, 128), F32),
            pltpu.VMEM((256, 256), BF16),
            pltpu.VMEM((2, 2, 4, 4, 16, 512), BF16),
            pltpu.VMEM((2, 2, 4, 4, 16, 512), BF16),
            pltpu.VMEM((2, 2, 4, 16, 512), BF16),
            pltpu.VMEM((2, 2, 4, 16, 512), BF16),
            pltpu.VMEM((16, 16, 128), F32),
            pltpu.VMEM((16, 16, 128), BF16),
            pltpu.VMEM((16, 16, 128), BF16),
            pltpu.SemaphoreType.DMA((19, 16)),
            pltpu.SemaphoreType.DMA((19, 16)),
            pltpu.SemaphoreType.DMA((32,)),
        ],
        compiler_params=pltpu.CompilerParams(
            collective_id=0, has_side_effects=True, vmem_limit_bytes=48 * 1024 * 1024
        ),
        name="layer",
    )(*(
        pltpu.with_memory_space_constraint(operand, pltpu.HBM) for operand in (
            x_stream, z_stream, conv_state.transpose(1, 0, 2), conv_weight, conv_bias[None], x_weight.T,
            dt_bias[None], a_log, skip_gain[None], norm_gain[None], route_ids.T, route_weights.T, hidden_in,
            dt_weight, ssm_state, out_weight, gate_proj, up_proj, down_proj,
        )
    ))
    row, new_conv_state, new_ssm_state = pl.pallas_call(
        finish_kernel,
        out_shape=(
            jax.ShapeDtypeStruct((1, 4096), BF16),
            jax.ShapeDtypeStruct((3, 16, 512), BF16),
            jax.ShapeDtypeStruct((16, 16, 512), F32),
        ),
        in_specs=[vmem] * 3,
        out_specs=(vmem, hbm, hbm),
        scratch_shapes=[pltpu.SemaphoreType.DMA((5,))],
        compiler_params=pltpu.CompilerParams(vmem_limit_bytes=48 * 1024 * 1024),
        name="finish",
    )(row, new_conv_state, new_ssm_state)
    return (row, new_conv_state.transpose(1, 0, 2), new_ssm_state)


def solution(mesh):
    return jax.shard_map(
        local,
        mesh=mesh,
        in_specs=(
            P(("expert", "tensor"), None),
            P("expert", "tensor"),
            P("expert", "tensor"),
            P("expert", None, "tensor"),
            P("expert", None, "tensor"),
            P(None, "tensor"),
            P("tensor"),
            P("tensor", None),
            P(None, "tensor"),
            P("tensor"),
            P(None, "tensor"),
            P("tensor"),
            P("tensor", "expert", None),
            P(),
            P(),
            P(),
            P("expert", None, "tensor"),
            P("expert", None, "tensor"),
            P("expert", "tensor", None),
        ),
        out_specs=(
            P(("expert", "tensor"), None),
            P("expert", None, "tensor"),
            P("expert", None, "tensor"),
        ),
        check_vma=False,
    )
```

```python
import jax
import jax.numpy as jnp
from jax import lax
from jax.experimental import pallas as pl
from jax.experimental.pallas import tpu as pltpu
from jax.sharding import PartitionSpec as P

F32 = jnp.float32
BF16 = jnp.bfloat16
MESH = pl.DeviceIdType.MESH

(
    PROJ, WOUT_M, WOUT, HID_M, HID, DOWN_M, MIX, MIX_M, OUTRED, RESID, STAT, SCALE,
    ROWS1, ROWS2, ROWS3, ACT, RED1, RED2, FINAL,
) = range(19)


def layer_kernel(
    x_hbm, z_hbm, cs_hbm, cw_hbm, cb_hbm, xw_hbm, dtb_hbm, alog_hbm, skip_hbm, gain_hbm, ids_hbm, rw_hbm, hid_hbm,
    dtw_hbm, ssm_hbm, ow_hbm, gate_hbm, up_hbm, down_hbm,
    out_ref, ncs_ref, nssm_ref,
    x_ref, z_ref, cs_ref, cw_ref, cb_ref, xw_ref, dtb_ref, alog_ref, skip_ref, gain_ref, ids_ref, rw_ref, hid_ref,
    dtw, ssm, wg, wu, wd, wd_mate, owh, ow,
    proj, proj_in, hid_out, hidh, hid_in, readout, mix, outb, outr, res, stat, scales, resrow, xn, acc_g, acc_u,
    actw, act_mate, wrow, perm, own, red1, tsum, red2, vrow, vsend, final_in,
    ssem, rsem, lsem,
):
    e = lax.axis_index("expert")
    t = lax.axis_index("tensor")
    y, x = lax.div(t, 4), lax.rem(t, 4)
    z, c = lax.div(e, 2), lax.rem(e, 2)
    m = 1 - c
    mate = 2 * z + m
    q0, q1 = 2 * c, 2 * c + 1
    p0 = 2 * m

    def rcopy(src, dst, phase, to, frm, device):
        return pltpu.make_async_remote_copy(
            src_ref=src, dst_ref=dst, send_sem=ssem.at[phase, to], recv_sem=rsem.at[phase, frm],
            device_id=device, device_id_type=MESH,
        )

    def others(n, me, body):
        def step(d, carry):
            body(lax.rem(me + (5 * d if n == 16 else 3 * d if n == 8 else 3 - d + lax.div(d, 3) * 3), n))
            return carry
        lax.fori_loop(1, n, step, 0)

    def at_z(o):
        return (2 * o + c, t)

    def at_x(o):
        return (e, y * 4 + o)

    def at_y(o):
        return (e, o * 4 + x)

    def half(which):
        return pl.ds(pl.multiple_of(which * 2048, 2048), 2048)

    def lcopy(src, dst, i):
        return pltpu.make_async_copy(src, dst, lsem.at[i])

    early = [
        lcopy(src, dst, i) for i, (src, dst) in enumerate((
            (x_hbm, x_ref), (cs_hbm, cs_ref), (cw_hbm, cw_ref), (cb_hbm, cb_ref),
        ))
    ]
    later = [
        lcopy(src, dst, 5 + i) for i, (src, dst) in enumerate((
            (hid_hbm, hid_ref), (dtw_hbm, dtw), (ssm_hbm, ssm), (ids_hbm, ids_ref), (rw_hbm, rw_ref),
            (z_hbm, z_ref), (dtb_hbm, dtb_ref), (alog_hbm, alog_ref), (skip_hbm, skip_ref), (gain_hbm, gain_ref),
        ))
    ]
    weights = []
    for q in range(4):
        weights.append(lcopy(gate_hbm.at[0, pl.ds(q * 1024, 1024), :], wg.at[q], 16 + q))
        weights.append(lcopy(up_hbm.at[0, pl.ds(q * 1024, 1024), :], wu.at[q], 20 + q))

    def down_cols(which, s):
        return down_hbm.at[0, :, pl.ds(pl.multiple_of(which * 2048 + s * 1024, 1024), 1024)]

    for s in range(2):
        weights.append(lcopy(down_cols(c, s), wd.at[s], 24 + s))
    for k in range(4):
        part = pl.ds(k * 128, 128 if k < 3 else 160)
        early.append(lcopy(xw_hbm.at[part], xw_ref.at[part], 28 + k))
    own_weight = lcopy(ow_hbm.at[0, :, half(c)], owh.at[c], 15)
    for copy in early:
        copy.start()
    own_weight.start()

    def greet(device):
        pl.semaphore_signal(bar, inc=1, device_id=device, device_id_type=MESH)

    bar = pltpu.get_barrier_semaphore()
    others(16, t, lambda o: greet((e, o)))
    others(8, z, lambda o: greet(at_z(o)))
    greet((mate, t))

    for copy in early:
        copy.wait()
    state = cs_ref[...].astype(F32)
    taps = cw_ref[...].astype(F32)
    newest = x_ref[...].astype(F32)
    window = [state[0], state[1], state[2], newest]
    conv_sum = sum(window[k] * taps[k : k + 1, :] for k in range(4)) + cb_ref[...]
    conv_out = jax.nn.silu(conv_sum).astype(BF16)
    inputs = conv_out.astype(F32)
    part = lax.dot_general(
        conv_out, xw_ref[...], (((1,), (1,)), ((), ())), preferred_element_type=F32
    )
    proj[...] = jnp.zeros((16, 640), BF16)
    proj[:, 0:544] = part.astype(BF16)

    pl.semaphore_wait(bar, 23)

    def wout_copy(o):
        cols = pl.ds(pl.multiple_of(o * 256, 256), 256)
        return rcopy(owh.at[:, :, cols], ow.at[z], WOUT, o, z, at_z(o))

    def wout_from(o):
        return rcopy(ow.at[o], ow.at[o], WOUT, o, o, at_z(o))

    def proj_copy(o):
        return rcopy(proj, proj_in.at[t], PROJ, o, t, (e, o))

    wout_mate = rcopy(ow_hbm.at[0, :, half(m)], owh.at[c], WOUT_M, 0, 0, (mate, t))
    wout_from_mate = rcopy(ow_hbm.at[0, :, half(m)], owh.at[m], WOUT_M, 0, 0, (mate, t))
    wout_mate.start()
    others(16, t, lambda o: proj_copy(o).start())
    proj_in[t] = proj[...]
    wout_from_mate.wait_recv()
    own_weight.wait()
    others(8, z, lambda o: wout_copy(o).start())

    hid_mate = rcopy(hid_out.at[pl.ds(8 * m, 8)], hidh.at[:, c], HID_M, 0, 0, (mate, t))
    hid_from_mate = rcopy(hid_out.at[pl.ds(8 * m, 8)], hidh.at[:, m], HID_M, 0, 0, (mate, t))

    def down_mate(s):
        return rcopy(down_cols(m, s), wd_mate.at[s], DOWN_M, s, s, (mate, t))

    for copy in later:
        copy.start()
    for copy in weights:
        copy.start()
    for copy in later:
        copy.wait()
    hidden = hid_ref[...].astype(F32)
    for k in range(16):
        hid_out[k] = hidden[:, 256 * k : 256 * (k + 1)]
    hid_mate.start()
    hidh[:, c] = hid_out[pl.ds(8 * c, 8)]
    ncs_ref[0] = cs_ref[1]
    ncs_ref[1] = cs_ref[2]
    ncs_ref[2] = x_ref[...]

    ow[z] = owh[:, :, pl.ds(pl.multiple_of(z * 256, 256), 256)]

    def hid_copy(o):
        return rcopy(hidh.at[o], hid_in.at[z], HID, o, z, at_z(o))

    def hid_from(o):
        return rcopy(hidh.at[o], hid_in.at[o], HID, o, o, at_z(o))

    row = lax.broadcasted_iota(jnp.int32, (256, 256), 0)
    col = lax.broadcasted_iota(jnp.int32, (256, 256), 1)
    chosen = col == lax.rem(row, 16) * 16 + lax.div(row, 16)
    perm[...] = jnp.where(chosen, 1.0, 0.0).astype(BF16)
    hit = jnp.sum(jnp.where(ids_ref[...] == z, rw_ref[...], 0.0), axis=0, keepdims=True)
    picked = jnp.sum(jnp.where(chosen, hit, 0.0), axis=1, keepdims=True)
    wrow[...] = jnp.broadcast_to(picked, (256, 128))
    decay = -jnp.exp(alog_ref[...])
    gate_z = jax.nn.silu(z_ref[...].astype(F32))
    wout_mate.wait_send()
    hid_mate.wait_send()

    others(16, t, lambda o: rcopy(proj, proj_in.at[o], PROJ, o, o, (e, o)).wait_recv())
    total = jnp.sum(proj_in[...].astype(F32), axis=0)

    step_size = jax.nn.softplus(
        jnp.dot(total[:, 0:512].astype(BF16), dtw[...], preferred_element_type=F32) + dtb_ref[...]
    )
    maps = total[:, 512:640].T
    b_map, c_map = maps[0:16, :], maps[16:32, :]
    driven = step_size * inputs
    for r in range(16):
        new = jnp.exp(step_size[r : r + 1, :] * decay) * ssm[r] + driven[r : r + 1, :] * b_map[:, r : r + 1]
        nssm_ref[r] = new
        readout[r : r + 1, :] = jnp.sum(new * c_map[:, r : r + 1], axis=0, keepdims=True)
    mix[e] = ((readout[...] + skip_ref[...] * inputs) * gate_z).astype(BF16)

    def mix_copy(o):
        return rcopy(mix.at[e], mix.at[e], MIX, o, z, at_z(o))

    def mix_from(o):
        return rcopy(mix.at[2 * o + c], mix.at[2 * o + c], MIX, o, o, at_z(o))

    def mix_to_mate(o):
        return rcopy(mix.at[2 * o + c], mix.at[2 * o + c], MIX_M, o, o, (mate, t))

    def mix_from_mate(o):
        return rcopy(mix.at[2 * o + m], mix.at[2 * o + m], MIX_M, o, o, (mate, t))

    others(8, z, lambda o: mix_copy(o).start())
    mix_to_mate(z).start()
    hid_from_mate.wait_recv()
    others(8, z, lambda o: hid_copy(o).start())
    hid_in[z] = hidh[z]
    others(8, z, lambda o: wout_from(o).wait_recv())

    def mix_pass(o):
        mix_from(o).wait_recv()
        mix_to_mate(o).start()

    others(8, z, mix_pass)
    mix_from_mate(z).wait_recv()
    others(8, z, lambda o: mix_from_mate(o).wait_recv())
    ordered = jnp.dot(perm[...], mix[...].reshape(256, 512), preferred_element_type=F32).astype(BF16)
    mixed = jnp.dot(ordered, ow[...].reshape(512, 256), preferred_element_type=F32)
    outb[...] = mixed.astype(BF16).reshape(16, 16, 256)

    def out_copy(o):
        return rcopy(outb.at[o], outr.at[t], OUTRED, o, t, (e, o))

    others(16, t, lambda o: out_copy(o).start())
    outr[t] = outb[t]
    down_mate(0).start()
    down_mate(1).start()
    others(16, t, lambda o: proj_copy(o).wait_send())
    others(8, z, lambda o: wout_copy(o).wait_send())
    others(8, z, lambda o: hid_copy(o).wait_send())
    others(8, z, lambda o: hid_from(o).wait_recv())
    others(8, z, lambda o: mix_copy(o).wait_send())
    mix_to_mate(z).wait_send()
    others(8, z, lambda o: mix_to_mate(o).wait_send())
    others(16, t, lambda o: rcopy(outb.at[o], outr.at[o], OUTRED, o, o, (e, o)).wait_recv())
    res[z] = (jnp.sum(outr[...].astype(F32), axis=0) + hid_in[...].reshape(16, 256)).astype(BF16)

    def res_copy(o):
        return rcopy(res.at[z], res.at[z], RESID, o, z, at_z(o))

    others(8, z, lambda o: res_copy(o).start())
    others(16, t, lambda o: out_copy(o).wait_send())
    others(8, z, lambda o: rcopy(res.at[o], res.at[o], RESID, o, o, at_z(o)).wait_recv())
    for b in range(8):
        gain = gain_ref[:, pl.ds(pl.multiple_of(c * 2048 + b * 256, 256), 256)]
        value = (res[b].astype(F32) * gain).astype(BF16)
        xn[2 * c + b // 4, y, x, :, (b % 4) * 256 : (b % 4 + 1) * 256] = value

    def rows1_x(o, frm):
        return rcopy(xn.at[q0, y, x], xn.at[q0, y, frm], ROWS1, o, frm, at_x(o))

    def rows1_y(o, frm):
        return rcopy(xn.at[q1, y, x], xn.at[q1, frm, x], ROWS1, 4 + o, 4 + frm, at_y(o))

    def rows2_y(o, frm):
        return rcopy(xn.at[q0, y], xn.at[q0, frm], ROWS2, o, frm, at_y(o))

    def rows2_x(o, frm):
        return rcopy(xn.at[q1, :, x], xn.at[q1, :, frm], ROWS2, 4 + o, 4 + frm, at_x(o))

    def pass_y(bx, o):
        return rcopy(xn.at[q0, y, bx], xn.at[q0, y, bx], ROWS2, o, y, at_y(o))

    def pass_x(by, o):
        return rcopy(xn.at[q1, by, x], xn.at[q1, by, x], ROWS2, 4 + o, 4 + x, at_x(o))

    def rows3_0(q, o):
        return rcopy(xn.at[q, o], xn.at[q, o], ROWS3, o, o, (mate, t))

    def rows3_1(q, o):
        return rcopy(xn.at[q, :, o], xn.at[q, :, o], ROWS3, 4 + o, 4 + o, (mate, t))

    others(4, x, lambda o: rows1_x(o, x).start())
    others(4, y, lambda o: rows1_y(o, y).start())
    others(4, y, lambda o: pass_y(x, o).start())
    others(4, x, lambda o: pass_x(y, o).start())
    squares = jnp.zeros((16, 256), F32)
    for b in range(8):
        piece = res[b].astype(F32)
        squares = squares + piece * piece
    sums = jnp.broadcast_to(jnp.sum(squares, axis=1, keepdims=True), (16, 128)).T
    stat[0] = jnp.zeros((1, 128), F32)
    stat[0, :, 0:16] = sums[0:1, :]
    stat_copy = rcopy(stat.at[0], stat.at[1], STAT, 0, 0, (mate, t))
    stat_copy.start()
    others(8, z, lambda o: res_copy(o).wait_send())
    stat_copy.wait()
    scales[t] = lax.rsqrt((stat[0] + stat[1]) * (1.0 / 4096) + 1e-5)

    def scale_copy(o):
        return rcopy(scales.at[t], scales.at[t], SCALE, o, t, (e, o))

    others(16, t, lambda o: scale_copy(o).start())
    place = lax.broadcasted_iota(jnp.int32, (16, 256), 0)
    for k in range(2):
        mine = place == 2 * z + k
        for b in range(8):
            line = jnp.sum(jnp.where(mine, res[b].astype(F32), 0.0), axis=0, keepdims=True)
            resrow[k, 2 * b : 2 * b + 1, :] = line[:, 0:128]
            resrow[k, 2 * b + 1 : 2 * b + 2, :] = line[:, 128:256]

    def line_pass(d, carry):
        bx, by = lax.rem(x + 4 - d, 4), lax.rem(y + 4 - d, 4)
        rows1_x(bx, bx).wait_recv()
        others(4, y, lambda o: pass_y(bx, o).start())
        rows1_y(by, by).wait_recv()
        others(4, x, lambda o: pass_x(by, o).start())
        return carry

    lax.fori_loop(1, 4, line_pass, 0)
    rows3_0(q0, y).start()
    rows3_1(q1, x).start()
    for copy in weights:
        copy.wait()
    for s in range(2):
        down_mate(s).wait()
    others(4, x, lambda o: rows1_x(o, x).wait_send())
    others(4, y, lambda o: rows1_y(o, y).wait_send())

    def forward(d, carry):
        oy, ox = lax.rem(y + 4 - d, 4), lax.rem(x + 4 - d, 4)
        rows2_y(oy, oy).wait_recv()
        rows3_0(q0, oy).start()
        rows2_x(ox, ox).wait_recv()
        rows3_1(q1, ox).start()
        return carry

    lax.fori_loop(1, 4, forward, 0)

    acc_g[...] = jnp.zeros((256, 384), F32)
    acc_u[...] = jnp.zeros((256, 384), F32)

    def project(q):
        rows = xn[q].reshape(256, 1024)
        acc_g[...] += jnp.dot(rows, wg[q], preferred_element_type=F32)
        acc_u[...] += jnp.dot(rows, wu[q], preferred_element_type=F32)

    def project_half(first):
        def step(s, carry):
            project(first + s)
            return carry
        lax.fori_loop(0, 2, step, 0)

    project_half(q0)

    others(16, t, lambda o: rcopy(scales.at[o], scales.at[o], SCALE, o, o, (e, o)).wait_recv())
    lane = lax.broadcasted_iota(jnp.int32, (16, 16, 128), 2)
    slot = lax.broadcasted_iota(jnp.int32, (16, 16, 128), 1)
    picked = jnp.where(lane == slot, jnp.broadcast_to(scales[...], (16, 16, 128)), 0.0).reshape(256, 128)
    scale = jnp.broadcast_to(jnp.sum(picked, axis=1, keepdims=True), (256, 384))

    def mate_rows(o, carry):
        rows3_0(p0, o).wait_recv()
        rows3_1(p0 + 1, o).wait_recv()
        return carry

    lax.fori_loop(0, 4, mate_rows, 0)
    project_half(p0)
    weight = jnp.concatenate([wrow[...]] * 3, axis=1)
    actw[...] = (jax.nn.silu(acc_g[...] * scale) * (acc_u[...] * scale) * weight).astype(BF16)

    act_copy = rcopy(actw, act_mate, ACT, 0, 0, (mate, t))
    act_copy.start()

    def red1_copy(s, h, o, frm):
        if s == 0:
            return rcopy(own.at[0, h, :, o], red1.at[0, h, frm], RED1, 4 * h + o, 4 * h + frm, at_x(o))
        return rcopy(own.at[1, h, o], red1.at[1, h, frm], RED1, 8 + 4 * h + o, 8 + 4 * h + frm, at_y(o))

    def red2_copy(s, h, o, frm):
        if s == 0:
            return rcopy(tsum.at[0, h, o], red2.at[0, h, frm], RED2, 4 * h + o, 4 * h + frm, at_y(o))
        return rcopy(tsum.at[1, h, o], red2.at[1, h, frm], RED2, 8 + 4 * h + o, 8 + 4 * h + frm, at_x(o))

    one, two = (x, y), (y, x)

    def down(s, h, act, weight):
        return jnp.dot(act[...], weight[s, :, 512 * h : 512 * (h + 1)], preferred_element_type=F32)

    parts = [(0, 0), (1, 0), (0, 1), (1, 1)]
    for s, h in parts:
        value = down(s, h, actw, wd)
        if (s, h) == (0, 0):
            act_copy.wait()
        value = value + down(s, h, act_mate, wd_mate)
        own[s, h] = value.astype(BF16).reshape(4, 4, 16, 512)
        others(4, one[s], lambda o: red1_copy(s, h, o, one[s]).start())

    others(16, t, lambda o: scale_copy(o).wait_send())
    others(4, y, lambda o: rows2_y(o, y).wait_send())
    others(4, x, lambda o: rows2_x(o, x).wait_send())

    def rows3_sent(o, carry):
        rows3_0(q0, o).wait_send()
        rows3_1(q1, o).wait_send()
        return carry

    lax.fori_loop(0, 4, rows3_sent, 0)

    for s, h in parts:
        others(4, one[s], lambda o: red1_copy(s, h, o, o).wait_recv())
        value = (own[0, h, :, x] if s == 0 else own[1, h, y]).astype(F32)
        for d in range(1, 4):
            value = value + red1[s, h, lax.rem(one[s] + d, 4)].astype(F32)
        tsum[s, h] = value.astype(BF16)
        others(4, two[s], lambda o: red2_copy(s, h, o, two[s]).start())
    for s, h in parts:
        others(4, one[s], lambda o: red1_copy(s, h, o, one[s]).wait_send())

    for s, h in parts:
        others(4, two[s], lambda o: red2_copy(s, h, o, o).wait_recv())
        value = tsum[s, h, two[s]].astype(F32)
        for d in range(1, 4):
            value = value + red2[s, h, lax.rem(two[s] + d, 4)].astype(F32)
        for k in range(4):
            vrow[:, 8 * s + 4 * h + k, :] = value[:, 128 * k : 128 * (k + 1)]

    vrow[pl.ds(2 * z, 2)] += resrow[...]
    vsend[...] = vrow[...].astype(BF16)

    def final_copy(o):
        return rcopy(vsend.at[o], final_in.at[e], FINAL, o, e, (o, t))

    others(16, e, lambda o: final_copy(o).start())
    final_in[e] = vsend[e]
    for s, h in parts:
        others(4, two[s], lambda o: red2_copy(s, h, o, two[s]).wait_send())
    others(16, e, lambda o: rcopy(vsend.at[o], final_in.at[o], FINAL, o, o, (o, t)).wait_recv())
    for k in range(2):
        value = final_in[k].astype(F32)
        for b in range(1, 8):
            value = value + final_in[2 * b + k].astype(F32)
        for b in range(16):
            out_ref[:, 2048 * k + 128 * b : 2048 * k + 128 * (b + 1)] = value[b : b + 1, :]
    others(16, e, lambda o: final_copy(o).wait_send())


def finish_kernel(row, ncs, nssm, row_out, ncs_out, nssm_out, sem):
    copies = [
        pltpu.make_async_copy(nssm.at[pl.ds(4 * k, 4)], nssm_out.at[pl.ds(4 * k, 4)], sem.at[k]) for k in range(4)
    ]
    copies.append(pltpu.make_async_copy(ncs, ncs_out, sem.at[4]))
    for copy in copies:
        copy.start()
    row_out[...] = row[...].astype(BF16)
    for copy in copies:
        copy.wait()


def local(
    hidden_in,
    x_stream,
    z_stream,
    conv_state,
    ssm_state,
    conv_weight,
    conv_bias,
    x_weight,
    dt_weight,
    dt_bias,
    a_log,
    skip_gain,
    out_weight,
    norm_gain,
    route_ids,
    route_weights,
    gate_proj,
    up_proj,
    down_proj,
):
    vmem = pl.BlockSpec(memory_space=pltpu.VMEM)
    hbm = pl.BlockSpec(memory_space=pltpu.HBM)
    row, new_conv_state, new_ssm_state = pl.pallas_call(
        layer_kernel,
        out_shape=(
            pltpu.VMEM((1, 4096), F32),
            pltpu.VMEM((3, 16, 512), BF16),
            pltpu.VMEM((16, 16, 512), F32),
        ),
        in_specs=[hbm] * 19,
        out_specs=(vmem, vmem, vmem),
        scratch_shapes=[
            pltpu.VMEM((16, 512), BF16),
            pltpu.VMEM((16, 512), BF16),
            pltpu.VMEM((3, 16, 512), BF16),
            pltpu.VMEM((4, 512), BF16),
            pltpu.VMEM((1, 512), F32),
            pltpu.VMEM((544, 512), BF16),
            pltpu.VMEM((1, 512), F32),
            pltpu.VMEM((16, 512), F32),
            pltpu.VMEM((1, 512), F32),
            pltpu.VMEM((1, 4096), F32),
            pltpu.VMEM((2, 256), jnp.int32),
            pltpu.VMEM((2, 256), F32),
            pltpu.VMEM((1, 4096), BF16),
            pltpu.VMEM((512, 512), BF16),
            pltpu.VMEM((16, 16, 512), F32),
            pltpu.VMEM((4, 1024, 384), BF16),
            pltpu.VMEM((4, 1024, 384), BF16),
            pltpu.VMEM((2, 384, 1024), BF16),
            pltpu.VMEM((2, 384, 1024), BF16),
            pltpu.VMEM((2, 32, 2048), BF16),
            pltpu.VMEM((8, 2, 32, 256), BF16),
            pltpu.VMEM((16, 640), BF16),
            pltpu.VMEM((16, 16, 640), BF16),
            pltpu.VMEM((16, 1, 256), F32),
            pltpu.VMEM((8, 2, 1, 256), F32),
            pltpu.VMEM((8, 2, 1, 256), F32),
            pltpu.VMEM((16, 512), F32),
            pltpu.VMEM((16, 16, 512), BF16),
            pltpu.VMEM((16, 16, 256), BF16),
            pltpu.VMEM((16, 16, 256), BF16),
            pltpu.VMEM((8, 16, 256), BF16),
            pltpu.VMEM((2, 1, 128), F32),
            pltpu.VMEM((16, 1, 128), F32),
            pltpu.VMEM((2, 16, 128), F32),
            pltpu.VMEM((4, 4, 4, 16, 1024), BF16),
            pltpu.VMEM((256, 384), F32),
            pltpu.VMEM((256, 384), F32),
            pltpu.VMEM((256, 384), BF16),
            pltpu.VMEM((256, 384), BF16),
            pltpu.VMEM((256, 128), F32),
            pltpu.VMEM((256, 256), BF16),
            pltpu.VMEM((2, 2, 4, 4, 16, 512), BF16),
            pltpu.VMEM((2, 2, 4, 4, 16, 512), BF16),
            pltpu.VMEM((2, 2, 4, 16, 512), BF16),
            pltpu.VMEM((2, 2, 4, 16, 512), BF16),
            pltpu.VMEM((16, 16, 128), F32),
            pltpu.VMEM((16, 16, 128), BF16),
            pltpu.VMEM((16, 16, 128), BF16),
            pltpu.SemaphoreType.DMA((19, 16)),
            pltpu.SemaphoreType.DMA((19, 16)),
            pltpu.SemaphoreType.DMA((32,)),
        ],
        compiler_params=pltpu.CompilerParams(
            collective_id=0, has_side_effects=True, vmem_limit_bytes=48 * 1024 * 1024
        ),
        name="layer",
    )(*(
        pltpu.with_memory_space_constraint(operand, pltpu.HBM) for operand in (
            x_stream, z_stream, conv_state.transpose(1, 0, 2), conv_weight, conv_bias[None], x_weight.T,
            dt_bias[None], a_log, skip_gain[None], norm_gain[None], route_ids.T, route_weights.T, hidden_in,
            dt_weight, ssm_state, out_weight, gate_proj, up_proj, down_proj,
        )
    ))
    row, new_conv_state, new_ssm_state = pl.pallas_call(
        finish_kernel,
        out_shape=(
            jax.ShapeDtypeStruct((1, 4096), BF16),
            jax.ShapeDtypeStruct((3, 16, 512), BF16),
            jax.ShapeDtypeStruct((16, 16, 512), F32),
        ),
        in_specs=[vmem] * 3,
        out_specs=(vmem, hbm, hbm),
        scratch_shapes=[pltpu.SemaphoreType.DMA((5,))],
        compiler_params=pltpu.CompilerParams(vmem_limit_bytes=48 * 1024 * 1024),
        name="finish",
    )(row, new_conv_state, new_ssm_state)
    return (row, new_conv_state.transpose(1, 0, 2), new_ssm_state)


def solution(mesh):
    return jax.shard_map(
        local,
        mesh=mesh,
        in_specs=(
            P(("expert", "tensor"), None),
            P("expert", "tensor"),
            P("expert", "tensor"),
            P("expert", None, "tensor"),
            P("expert", None, "tensor"),
            P(None, "tensor"),
            P("tensor"),
            P("tensor", None),
            P(None, "tensor"),
            P("tensor"),
            P(None, "tensor"),
            P("tensor"),
            P("tensor", "expert", None),
            P(),
            P(),
            P(),
            P("expert", None, "tensor"),
            P("expert", None, "tensor"),
            P("expert", "tensor", None),
        ),
        out_specs=(
            P(("expert", "tensor"), None),
            P("expert", None, "tensor"),
            P("expert", None, "tensor"),
        ),
        check_vma=False,
    )
```
